512 devices in a mesh: rep: 16 (over y, x_lo), fsdp: 32 (over x_hi, z, core).
Axes of the slice: x: 4 (x_hi: 2, x_lo: 2; x = x_hi * 2 + x_lo), y: 8, z: 8, core: 2. Of those that a mesh axis runs over, the one named last changes fastest.
Arguments:
- pseudo_grad: float32 [16, 16384, 256], P('rep', 'fsdp'), may hold values from -6 to 6
- error_buf: float32 [16, 16384, 256], P('rep', 'fsdp'), may hold values from -6 to 6
- momentum: float32 [16384, 256], P('fsdp'), may hold values from -4 to 4
- params: float32 [16384, 256], P('fsdp'), may hold values from -6 to 6
- picks: int32 [16, 256], P('rep', 'fsdp'), may hold values from 0 to 511, as said below
Outputs:
- new_params: float32 [16384, 256], P('fsdp')
- new_momentum: float32 [16384, 256], P('fsdp')
- new_error: float32 [16, 16384, 256], P('rep', 'fsdp')
- gathered: bfloat16 [16384, 256], replicated
The draws below stay inside these ranges and needn't reach their ends.
Inputs may be any that keep to these rules, and one draw needn't show every extreme that they name: `picks`: entries j of a row with the same j // 8 are distinct.
All inputs are finite; a program needn't handle non-finite values.
Results may differ from the reference program's by a relative error of at most 0.0017.
Values may be sent and summed in bfloat16 or wider, within the bound.
No kernel may reach another device: no remote copies, remote signals or barrier semaphores. Data moves between devices by JAX's collectives and lax.ppermute only.
A program may use at most 64 MiB of HBM per device.

```python
import jax
import jax.numpy as jnp

BLOCK = 256
BLOCKS_DEV = 512
TOPK = 8
REPLICAS = 16
BLOCKS = 16384
TOPK_ALL = 256
N_FSDP = 32


def draw_picks(key, part):
    key = jax.random.fold_in(key, 11)
    shard_count = REPLICAS * N_FSDP
    keys = jax.random.split(key, shard_count)
    inner = jax.vmap(lambda single: 1 + jax.random.permutation(single, BLOCKS_DEV - 2)[:TOPK])(keys)
    special = jax.random.randint(jax.random.fold_in(key, 1), (), 0, shard_count)
    forced = (jnp.arange(shard_count) == special)[:, None]
    column = jnp.arange(TOPK)[None, :]
    inner = jnp.where(forced & (column == 0), BLOCKS_DEV - 1, inner)
    inner = jnp.where(forced & (column == 1), 0, inner)
    return inner.reshape(REPLICAS, TOPK_ALL).astype(jnp.int32)


def shard_levels(stream_key, extent, shards, least, high):
    factor_of = 1.0
    for axis_at, shards_of in shards:
        steps = jax.random.uniform(jax.random.fold_in(jax.random.fold_in(stream_key, 6), axis_at), (shards_of,), jnp.float32, least / len(shards), high / len(shards))
        factor_of = factor_of * jnp.repeat(jnp.exp(steps), extent[axis_at] // shards_of).reshape((-1,) + (1,) * (len(extent) - 1 - axis_at))
    return factor_of


def noise(own_key, shape, scale, most, shards=(), kind=jnp.bfloat16):
    level = shard_levels(own_key, shape, shards, -0.22, 0.18) if shards else 1.0
    array = jax.random.normal(own_key, shape, jnp.float32) * scale * level
    return jnp.minimum(jnp.maximum(array, -most), most).astype(kind)


def setup_inputs(seed: int = 0) -> dict:
    splits = jax.random.split(jax.random.key(seed), 6)
    pseudo_grad = noise(splits[0], (REPLICAS, BLOCKS, BLOCK), 1.0, 6.0, ((0, 16), (1, 32)), jnp.float32)
    error_buf = noise(splits[1], (REPLICAS, BLOCKS, BLOCK), 1.0, 6.0, ((0, 16), (1, 32)), jnp.float32)
    momentum = noise(splits[2], (BLOCKS, BLOCK), 0.5, 4.0, ((0, 32),), jnp.float32)
    params = noise(splits[3], (BLOCKS, BLOCK), 1.0, 6.0, ((0, 32),), jnp.float32)
    picks = draw_picks(jax.random.fold_in(splits[5], 71), 0)
    return dict(pseudo_grad=pseudo_grad, error_buf=error_buf, momentum=momentum, params=params, picks=picks)


def reference(pseudo_grad, error_buf, momentum, params, picks):
    accumulated = 0.95 * error_buf + pseudo_grad
    owners = (jnp.arange(TOPK_ALL, dtype=jnp.int32) // TOPK) * BLOCKS_DEV
    global_picks = picks + owners[None, :]
    positions = jnp.arange(BLOCKS, dtype=jnp.int32)
    chosen = jnp.any(global_picks[:, :, None] == positions[None, None, :], axis=1).astype(jnp.float32)
    kept = accumulated * chosen[:, :, None]
    new_error = accumulated - kept
    delta = jnp.sum(kept, axis=0) / REPLICAS
    new_momentum = 0.9 * momentum + delta
    new_params = params - 0.7 * (delta + 0.9 * new_momentum)
    gathered = new_params.astype(jnp.bfloat16)
    return new_params, new_momentum, new_error, gathered
```

```python
import jax
import jax.numpy as jnp
from jax import lax
from jax.sharding import PartitionSpec as P

DECAY_RATE = 0.95
MOMENTUM_COEF = 0.9
STEP_SCALE = 0.7
LANES = 128


def per_device(pseudo_grad, error_buf, momentum, params, picks):
    shard_blocks, block = params.shape
    replicas = lax.axis_size("rep")
    own_picks = picks[0].astype(jnp.float32)
    topk = own_picks.shape[0]
    positions = lax.iota(jnp.float32, shard_blocks)
    accumulated = DECAY_RATE * error_buf[0] + pseudo_grad[0]
    selector = (own_picks[:, None] == positions[None, :]).astype(jnp.float32)
    chosen_values = jnp.dot(selector, accumulated, precision=lax.Precision.HIGHEST)
    payload = jnp.concatenate(
        [chosen_values, jnp.broadcast_to(own_picks[:, None], (topk, LANES))], axis=1
    )
    everyone = lax.all_to_all(
        jnp.broadcast_to(payload[None], (replicas, topk, block + LANES)), "rep", 0, 0
    ).reshape(replicas * topk, block + LANES)
    all_values, all_picks = everyone[:, :block], everyone[:, block]
    spread = (all_picks[:, None] == positions[None, :]).astype(jnp.float32)
    summed = lax.dot_general(
        spread, all_values, (((0,), (0,)), ((), ())), precision=lax.Precision.HIGHEST
    )
    delta = summed / replicas
    new_momentum = MOMENTUM_COEF * momentum + delta
    new_params = params - STEP_SCALE * (delta + MOMENTUM_COEF * new_momentum)
    gathered = lax.all_gather(new_params.astype(jnp.bfloat16), "fsdp", axis=0, tiled=True)
    chosen_mask = jnp.sum(selector, axis=0)
    new_error = (accumulated * (1.0 - chosen_mask)[:, None])[None]
    return (new_params, new_momentum, new_error, gathered)


def solution(mesh):
    in_specs = (
        P("rep", "fsdp", None),
        P("rep", "fsdp", None),
        P("fsdp", None),
        P("fsdp", None),
        P("rep", "fsdp"),
    )
    out_specs = (P("fsdp", None), P("fsdp", None), P("rep", "fsdp", None), P())
    return jax.shard_map(
        per_device, mesh=mesh, in_specs=in_specs, out_specs=out_specs, check_vma=False
    )
```

```python
import jax
import jax.numpy as jnp
from jax import lax
from jax.experimental import pallas as pl
from jax.experimental.pallas import tpu as pltpu
from jax.sharding import PartitionSpec as P

DECAY_RATE = 0.95
MOMENTUM_COEF = 0.9
STEP_SCALE = 0.7
LANES = 128
AXES = ("rep", "fsdp")
NX, NY, NZ, CORES = 4, 8, 8, 2
CLASSES = 2 * NZ
COLOURS = 4
VMEM_LIMIT = 40 * 1024 * 1024


def device_at(x, y, z, core):
    x, y, z, core = x % NX, y % NY, z % NZ, core % CORES
    return (y * 2 + x % 2) * (2 * NZ * CORES) + (x // 2) * (NZ * CORES) + z * CORES + core


PLACES = [
    (x, y, z, core) for x in range(NX) for y in range(NY) for z in range(NZ) for core in range(CORES)
]


def fetch(value, dx=0, dy=0, dz=0, dcore=0):
    pairs = [
        (device_at(x + dx, y + dy, z + dz, core + dcore), device_at(x, y, z, core))
        for x, y, z, core in PLACES
    ]
    return lax.ppermute(value, AXES, pairs)


def exchange_groups():
    groups = []
    for x in range(NX // 2):
        for y in range(NY):
            for core in range(CORES):
                pair = sorted((x, NX - 1 - x), key=lambda v: v // 2)
                groups.append([device_at(v, y, z, core) for v in pair for z in range(NZ)])
    return groups


def place_of_self():
    rep, shard = lax.axis_index("rep"), lax.axis_index("fsdp")
    x = (shard // (NZ * CORES)) * 2 + rep % 2
    return x, rep // 2, (shard // CORES) % NZ, shard % CORES


def colour_of(x, y, z):
    return (x + y + 2 * z) % COLOURS


def update_kernel(everyone, momentum, params, new_params, new_momentum, send, shard):
    blocks, block = params.shape
    entries = everyone.shape[0]
    values = everyone[:, :block]
    picks = everyone[:, block:]
    lane = lax.broadcasted_iota(jnp.int32, (entries, LANES), 1).astype(jnp.float32)
    spread = jnp.concatenate(
        [(picks == lane + float(at)).astype(jnp.bfloat16) for at in range(0, blocks, LANES)], axis=1
    )
    delta = jnp.zeros((blocks, block), jnp.float32)
    rest = values
    for _ in range(3):
        part = rest.astype(jnp.bfloat16)
        rest = rest - part.astype(jnp.float32)
        delta += lax.dot_general(
            spread, part, (((0,), (0,)), ((), ())), preferred_element_type=jnp.float32
        )
    delta = delta / 16.0
    momentum_now = MOMENTUM_COEF * momentum[...] + delta
    params_now = params[...] - STEP_SCALE * (delta + MOMENTUM_COEF * momentum_now)
    new_momentum[...] = momentum_now
    new_params[...] = params_now
    shard[...] = params_now.astype(jnp.bfloat16)
    x, y, z, core = place_of_self()
    rows = blocks // COLOURS
    for x_hi in range(2):
        x_there = lax.select(x // 2 == x_hi, x, NX - 1 - x)
        for z_there in range(NZ):
            start = pl.multiple_of(colour_of(x_there, y, z_there) * rows, rows)
            send[x_hi * NZ + z_there] = shard[pl.ds(start, rows), :]


def update(everyone, momentum, params):
    blocks, block = params.shape
    vmem = pl.BlockSpec(memory_space=pltpu.VMEM)
    return pl.pallas_call(
        update_kernel,
        out_shape=(
            jax.ShapeDtypeStruct((blocks, block), jnp.float32),
            jax.ShapeDtypeStruct((blocks, block), jnp.float32),
            jax.ShapeDtypeStruct((CLASSES, blocks // COLOURS, block), jnp.bfloat16),
        ),
        in_specs=[vmem] * 3,
        out_specs=(vmem,) * 3,
        scratch_shapes=[pltpu.VMEM((blocks, block), jnp.bfloat16)],
        compiler_params=pltpu.CompilerParams(vmem_limit_bytes=VMEM_LIMIT),
        cost_estimate=pl.CostEstimate(flops=10**8, bytes_accessed=4 * 10**6, transcendentals=0),
    )(everyone, momentum, params)


def put(whole, pieces, shape, dtype):
    arrays = []
    for piece in pieces:
        if not any(piece[0] is a for a in arrays):
            arrays.append(piece[0])
    slots = [next(i for i, a in enumerate(arrays) if a is piece[0]) for piece in pieces]
    given = [] if whole is None else [whole]

    def kernel(*refs):
        sources = refs[len(given) : len(given) + len(arrays)]
        out, sems = refs[-2:]
        x, y, z, core = place_of_self()
        copies = []
        for at, (piece, slot) in enumerate(zip(pieces, slots)):
            _, first, count, cls, other, offset = piece
            copies.append(
                pltpu.make_async_copy(
                    sources[slot].at[pl.ds(first, count)],
                    out.at[
                        pl.ds(cls, count),
                        1 - core if other else core,
                        (colour_of(x, y, z) + offset) % COLOURS,
                    ],
                    sems.at[at],
                )
            )
        for copy in copies:
            copy.start()
        for copy in copies:
            copy.wait()

    moved = sum(a.size for a in arrays) * 4
    return pl.pallas_call(
        kernel,
        out_shape=jax.ShapeDtypeStruct(shape, dtype),
        in_specs=[pl.BlockSpec(memory_space=pl.ANY)] * (len(given) + len(arrays)),
        out_specs=pl.BlockSpec(memory_space=pl.ANY),
        scratch_shapes=[pltpu.SemaphoreType.DMA((len(pieces),))],
        input_output_aliases={0: 0} if given else {},
        cost_estimate=pl.CostEstimate(flops=0, bytes_accessed=moved, transcendentals=0),
    )(*given, *arrays)


def gather_slab(send, rows, block):
    shape = (CLASSES, CORES, COLOURS, rows, block)
    half = CLASSES // 2
    own = lax.all_to_all(send, AXES, 0, 0, axis_index_groups=exchange_groups())
    low, high = own[:half], own[half:]
    first = [
        (fetch(low, dx=1), 0, 1),
        (fetch(high, dy=1), half, 1),
        (fetch(low, dx=-1), 0, -1),
    ]
    second = [
        (fetch(high, dy=-1), half, -1),
        (fetch(low, dz=1), 0, 2),
        (fetch(high, dz=-1), half, 2),
    ]
    own_there = fetch(own, dcore=1)
    whole = put(
        None,
        [(own, 0, CLASSES, 0, False, 0), (own_there, 0, CLASSES, 0, True, 0)],
        shape,
        send.dtype,
    )
    for batch in (first, second):
        joined = jnp.concatenate([piece for piece, _, _ in batch], axis=0)
        there = fetch(joined, dcore=1)
        pieces = [(joined, at * half, half, cls, False, off) for at, (_, cls, off) in enumerate(batch)]
        whole = put(whole, pieces, shape, send.dtype)
        pieces = [(there, at * half, half, cls, True, off) for at, (_, cls, off) in enumerate(batch)]
        whole = put(whole, pieces, shape, send.dtype)
    return whole


def per_device(pseudo_grad, error_buf, momentum, params, picks):
    blocks, block = params.shape
    replicas = lax.axis_size("rep")
    own_picks = picks[0].astype(jnp.float32)
    topk = own_picks.shape[0]
    positions = lax.iota(jnp.float32, blocks)
    accumulated = DECAY_RATE * error_buf[0] + pseudo_grad[0]
    selector = (own_picks[:, None] == positions[None, :]).astype(jnp.float32)
    chosen_values = jnp.dot(selector, accumulated, precision=lax.Precision.HIGHEST)
    payload = jnp.concatenate(
        [chosen_values, jnp.broadcast_to(own_picks[:, None], (topk, LANES))], axis=1
    )
    everyone = lax.all_to_all(
        jnp.broadcast_to(payload[None], (replicas, topk, block + LANES)), "rep", 0, 0
    ).reshape(replicas * topk, block + LANES)
    new_params, new_momentum, send = update(everyone, momentum, params)
    gathered = gather_slab(send, blocks // COLOURS, block)
    chosen_mask = jnp.sum(selector, axis=0)
    new_error = (accumulated * (1.0 - chosen_mask)[:, None])[None]
    return (new_params, new_momentum, new_error, gathered.reshape(-1, block))


def solution(mesh):
    in_specs = (
        P("rep", "fsdp", None),
        P("rep", "fsdp", None),
        P("fsdp", None),
        P("fsdp", None),
        P("rep", "fsdp"),
    )
    out_specs = (P("fsdp", None), P("fsdp", None), P("rep", "fsdp", None), P())
    return jax.shard_map(
        per_device, mesh=mesh, in_specs=in_specs, out_specs=out_specs, check_vma=False
    )
```

```python
import jax
import jax.numpy as jnp
from jax import lax
from jax.experimental import pallas as pl
from jax.experimental.pallas import tpu as pltpu
from jax.sharding import PartitionSpec as P

DECAY_RATE = 0.95
MOMENTUM_COEF = 0.9
STEP_SCALE = 0.7
LANES = 128
AXES = ("rep", "fsdp")
NX, NY, NZ, CORES = 4, 8, 8, 2
CLASSES = 2 * NZ
COLOURS = 4
VMEM_LIMIT = 40 * 1024 * 1024


def device_at(x, y, z, core):
    x, y, z, core = x % NX, y % NY, z % NZ, core % CORES
    return (y * 2 + x % 2) * (2 * NZ * CORES) + (x // 2) * (NZ * CORES) + z * CORES + core


PLACES = [
    (x, y, z, core) for x in range(NX) for y in range(NY) for z in range(NZ) for core in range(CORES)
]


def fetch(value, dx=0, dy=0, dz=0, dcore=0):
    pairs = [
        (device_at(x + dx, y + dy, z + dz, core + dcore), device_at(x, y, z, core))
        for x, y, z, core in PLACES
    ]
    return lax.ppermute(value, AXES, pairs)


def exchange_groups():
    groups = []
    for x in range(NX // 2):
        for y in range(NY):
            for core in range(CORES):
                pair = sorted((x, NX - 1 - x), key=lambda v: v // 2)
                groups.append([device_at(v, y, z, core) for v in pair for z in range(NZ)])
    return groups


def place_of_self():
    rep, shard = lax.axis_index("rep"), lax.axis_index("fsdp")
    x = (shard // (NZ * CORES)) * 2 + rep % 2
    return x, rep // 2, (shard // CORES) % NZ, shard % CORES


def colour_of(x, y, z):
    return (x + y + 2 * z) % COLOURS


def update_kernel(everyone, momentum, params, new_params, new_momentum, send, shard):
    blocks, block = params.shape
    entries = everyone.shape[0]
    values = everyone[:, :block]
    picks = everyone[:, block:]
    lane = lax.broadcasted_iota(jnp.int32, (entries, LANES), 1).astype(jnp.float32)
    spread = jnp.concatenate(
        [(picks == lane + float(at)).astype(jnp.bfloat16) for at in range(0, blocks, LANES)], axis=1
    )
    delta = jnp.zeros((blocks, block), jnp.float32)
    rest = values
    for _ in range(3):
        part = rest.astype(jnp.bfloat16)
        rest = rest - part.astype(jnp.float32)
        delta += lax.dot_general(
            spread, part, (((0,), (0,)), ((), ())), preferred_element_type=jnp.float32
        )
    delta = delta / 16.0
    momentum_now = MOMENTUM_COEF * momentum[...] + delta
    params_now = params[...] - STEP_SCALE * (delta + MOMENTUM_COEF * momentum_now)
    new_momentum[...] = momentum_now
    new_params[...] = params_now
    shard[...] = params_now.astype(jnp.bfloat16)
    x, y, z, core = place_of_self()
    rows = blocks // COLOURS
    for x_hi in range(2):
        x_there = lax.select(x // 2 == x_hi, x, NX - 1 - x)
        for z_there in range(NZ):
            start = pl.multiple_of(colour_of(x_there, y, z_there) * rows, rows)
            send[x_hi * NZ + z_there] = shard[pl.ds(start, rows), :]


def update(everyone, momentum, params):
    blocks, block = params.shape
    vmem = pl.BlockSpec(memory_space=pltpu.VMEM)
    return pl.pallas_call(
        update_kernel,
        out_shape=(
            jax.ShapeDtypeStruct((blocks, block), jnp.float32),
            jax.ShapeDtypeStruct((blocks, block), jnp.float32),
            jax.ShapeDtypeStruct((CLASSES, blocks // COLOURS, block), jnp.bfloat16),
        ),
        in_specs=[vmem] * 3,
        out_specs=(vmem,) * 3,
        scratch_shapes=[pltpu.VMEM((blocks, block), jnp.bfloat16)],
        compiler_params=pltpu.CompilerParams(vmem_limit_bytes=VMEM_LIMIT),
        cost_estimate=pl.CostEstimate(flops=10**8, bytes_accessed=4 * 10**6, transcendentals=0),
    )(everyone, momentum, params)


def put(whole, pieces, shape, dtype):
    arrays = []
    for piece in pieces:
        if not any(piece[0] is a for a in arrays):
            arrays.append(piece[0])
    slots = [next(i for i, a in enumerate(arrays) if a is piece[0]) for piece in pieces]
    given = [] if whole is None else [whole]

    def kernel(*refs):
        sources = refs[len(given) : len(given) + len(arrays)]
        out, sems = refs[-2:]
        x, y, z, core = place_of_self()
        copies = []
        for piece, slot in zip(pieces, slots):
            _, first, count, cls, other, offset = piece
            there = 1 - core if other else core
            colour = (colour_of(x, y, z) + offset) % COLOURS
            for at in range(count):
                copies.append(
                    pltpu.make_async_copy(
                        sources[slot].at[first + at],
                        out.at[cls + at, there, colour],
                        sems.at[len(copies)],
                    )
                )
        for copy in copies:
            copy.start()
        for copy in copies:
            copy.wait()

    total = sum(piece[2] for piece in pieces)
    moved = 4 * total * pieces[0][0][0].size
    return pl.pallas_call(
        kernel,
        out_shape=jax.ShapeDtypeStruct(shape, dtype),
        in_specs=[pl.BlockSpec(memory_space=pl.ANY)] * (len(given) + len(arrays)),
        out_specs=pl.BlockSpec(memory_space=pl.ANY),
        scratch_shapes=[pltpu.SemaphoreType.DMA((total,))],
        input_output_aliases={0: 0} if given else {},
        cost_estimate=pl.CostEstimate(flops=0, bytes_accessed=moved, transcendentals=0),
    )(*given, *arrays)


PERMUTES = (
    (dict(dx=1), 1, (0, 11)),
    (dict(dy=-1), -1, (0, 10)),
    (dict(dz=1), 2, (0, 9)),
    (dict(dz=-1), 2, (9, 16)),
    (dict(dx=-1), -1, (10, 16)),
    (dict(dy=1), 1, (11, 16)),
)
BATCHES = ((0, 1), (2, 3), (4, 5))


def gather_slab(send, rows, block):
    shape = (CLASSES, CORES, COLOURS, rows, block)
    own = lax.all_to_all(send, AXES, 0, 0, axis_index_groups=exchange_groups())
    arrived = [fetch(own[lo:hi], **where) for where, _, (lo, hi) in PERMUTES]
    own_there = fetch(own, dcore=1)
    whole = put(None, [(own, 0, CLASSES, 0, False, 0)], shape, send.dtype)
    whole = put(whole, [(own_there, 0, CLASSES, 0, True, 0)], shape, send.dtype)
    for batch in BATCHES:
        joined = jnp.concatenate([arrived[i] for i in batch], axis=0)
        there = fetch(joined, dcore=1)
        for array, other in ((joined, False), (there, True)):
            pieces, first = [], 0
            for i in batch:
                _, offset, (lo, hi) = PERMUTES[i]
                pieces.append((array, first, hi - lo, lo, other, offset))
                first += hi - lo
            whole = put(whole, pieces, shape, send.dtype)
    return whole


def per_device(pseudo_grad, error_buf, momentum, params, picks):
    blocks, block = params.shape
    replicas = lax.axis_size("rep")
    own_picks = picks[0].astype(jnp.float32)
    topk = own_picks.shape[0]
    positions = lax.iota(jnp.float32, blocks)
    accumulated = DECAY_RATE * error_buf[0] + pseudo_grad[0]
    selector = (own_picks[:, None] == positions[None, :]).astype(jnp.float32)
    chosen_values = jnp.dot(selector, accumulated, precision=lax.Precision.HIGHEST)
    payload = jnp.concatenate(
        [chosen_values, jnp.broadcast_to(own_picks[:, None], (topk, LANES))], axis=1
    )
    everyone = lax.all_to_all(
        jnp.broadcast_to(payload[None], (replicas, topk, block + LANES)), "rep", 0, 0
    ).reshape(replicas * topk, block + LANES)
    new_params, new_momentum, send = update(everyone, momentum, params)
    gathered = gather_slab(send, blocks // COLOURS, block)
    chosen_mask = jnp.sum(selector, axis=0)
    new_error = (accumulated * (1.0 - chosen_mask)[:, None])[None]
    return (new_params, new_momentum, new_error, gathered.reshape(-1, block))


def solution(mesh):
    in_specs = (
        P("rep", "fsdp", None),
        P("rep", "fsdp", None),
        P("fsdp", None),
        P("fsdp", None),
        P("rep", "fsdp"),
    )
    out_specs = (P("fsdp", None), P("fsdp", None), P("rep", "fsdp", None), P())
    return jax.shard_map(
        per_device, mesh=mesh, in_specs=in_specs, out_specs=out_specs, check_vma=False
    )
```

```python
import jax
import jax.numpy as jnp
from jax import lax
from jax.experimental import pallas as pl
from jax.experimental.pallas import tpu as pltpu
from jax.sharding import PartitionSpec as P

DECAY_RATE = 0.95
MOMENTUM_COEF = 0.9
STEP_SCALE = 0.7
LANES = 128
AXES = ("rep", "fsdp")
NX, NY, NZ, CORES = 4, 8, 8, 2
CLASSES = 2 * NZ
COLOURS = 4
VMEM_LIMIT = 40 * 1024 * 1024


def device_at(x, y, z, core):
    x, y, z, core = x % NX, y % NY, z % NZ, core % CORES
    return (y * 2 + x % 2) * (2 * NZ * CORES) + (x // 2) * (NZ * CORES) + z * CORES + core


PLACES = [
    (x, y, z, core) for x in range(NX) for y in range(NY) for z in range(NZ) for core in range(CORES)
]


def fetch(value, dx=0, dy=0, dz=0, dcore=0):
    pairs = [
        (device_at(x + dx, y + dy, z + dz, core + dcore), device_at(x, y, z, core))
        for x, y, z, core in PLACES
    ]
    return lax.ppermute(value, AXES, pairs)


def exchange_groups():
    groups = []
    for x in range(NX // 2):
        for y in range(NY):
            for core in range(CORES):
                pair = sorted((x, NX - 1 - x), key=lambda v: v // 2)
                groups.append([device_at(v, y, z, core) for v in pair for z in range(NZ)])
    return groups


def place_of_self():
    rep, shard = lax.axis_index("rep"), lax.axis_index("fsdp")
    x = (shard // (NZ * CORES)) * 2 + rep % 2
    return x, rep // 2, (shard // CORES) % NZ, shard % CORES


def colour_of(x, y, z):
    return (x + y + 2 * z) % COLOURS


def update_kernel(
    everyone, momentum_hbm, params_hbm, new_params, new_momentum, send, momentum, params, shard, sems
):
    blocks, block = params.shape
    loads = [
        pltpu.make_async_copy(momentum_hbm, momentum, sems.at[0]),
        pltpu.make_async_copy(params_hbm, params, sems.at[1]),
    ]
    for load in loads:
        load.start()
    entries = everyone.shape[0]
    values = everyone[:, :block]
    picks = everyone[:, block:]
    lane = lax.broadcasted_iota(jnp.int32, (entries, LANES), 1).astype(jnp.float32)
    spread = jnp.concatenate(
        [(picks == lane + float(at)).astype(jnp.bfloat16) for at in range(0, blocks, LANES)], axis=1
    )
    delta = jnp.zeros((blocks, block), jnp.float32)
    rest = values
    for _ in range(3):
        part = rest.astype(jnp.bfloat16)
        rest = rest - part.astype(jnp.float32)
        delta += lax.dot_general(
            spread, part, (((0,), (0,)), ((), ())), preferred_element_type=jnp.float32
        )
    delta = delta / 16.0
    for load in loads:
        load.wait()
    momentum_now = MOMENTUM_COEF * momentum[...] + delta
    params_now = params[...] - STEP_SCALE * (delta + MOMENTUM_COEF * momentum_now)
    new_momentum[...] = momentum_now
    new_params[...] = params_now
    shard[...] = params_now.astype(jnp.bfloat16)
    x, y, z, core = place_of_self()
    rows = blocks // COLOURS
    for x_hi in range(2):
        x_there = lax.select(x // 2 == x_hi, x, NX - 1 - x)
        for z_there in range(NZ):
            start = pl.multiple_of(colour_of(x_there, y, z_there) * rows, rows)
            send[x_hi * NZ + z_there] = shard[pl.ds(start, rows), :]


def update(everyone, momentum, params):
    blocks, block = params.shape
    vmem = pl.BlockSpec(memory_space=pltpu.VMEM)
    hbm = pl.BlockSpec(memory_space=pltpu.HBM)
    return pl.pallas_call(
        update_kernel,
        out_shape=(
            jax.ShapeDtypeStruct((blocks, block), jnp.float32),
            jax.ShapeDtypeStruct((blocks, block), jnp.float32),
            jax.ShapeDtypeStruct((CLASSES, blocks // COLOURS, block), jnp.bfloat16),
        ),
        in_specs=[vmem, hbm, hbm],
        out_specs=(vmem,) * 3,
        scratch_shapes=[
            pltpu.VMEM((blocks, block), jnp.float32),
            pltpu.VMEM((blocks, block), jnp.float32),
            pltpu.VMEM((blocks, block), jnp.bfloat16),
            pltpu.SemaphoreType.DMA((2,)),
        ],
        compiler_params=pltpu.CompilerParams(vmem_limit_bytes=VMEM_LIMIT),
        cost_estimate=pl.CostEstimate(flops=10**8, bytes_accessed=4 * 10**6, transcendentals=0),
    )(everyone, momentum, params)


def put(whole, pieces, shape, dtype):
    arrays = []
    for piece in pieces:
        if not any(piece[0] is a for a in arrays):
            arrays.append(piece[0])
    slots = [next(i for i, a in enumerate(arrays) if a is piece[0]) for piece in pieces]
    given = [] if whole is None else [whole]

    def kernel(*refs):
        sources = refs[len(given) : len(given) + len(arrays)]
        out, sems = refs[-2:]
        x, y, z, core = place_of_self()
        copies = []
        for piece, slot in zip(pieces, slots):
            _, first, count, cls, other, offset = piece
            there = 1 - core if other else core
            colour = (colour_of(x, y, z) + offset) % COLOURS
            for at in range(count):
                copies.append(
                    pltpu.make_async_copy(
                        sources[slot].at[first + at],
                        out.at[cls + at, there, colour],
                        sems.at[len(copies)],
                    )
                )
        for copy in copies:
            copy.start()
        for copy in copies:
            copy.wait()

    total = sum(piece[2] for piece in pieces)
    moved = 4 * total * pieces[0][0][0].size
    return pl.pallas_call(
        kernel,
        out_shape=jax.ShapeDtypeStruct(shape, dtype),
        in_specs=[pl.BlockSpec(memory_space=pltpu.HBM)] * len(given)
        + [pl.BlockSpec(memory_space=pltpu.VMEM)] * len(arrays),
        out_specs=pl.BlockSpec(memory_space=pltpu.HBM),
        scratch_shapes=[pltpu.SemaphoreType.DMA((total,))],
        input_output_aliases={0: 0} if given else {},
        compiler_params=pltpu.CompilerParams(vmem_limit_bytes=VMEM_LIMIT),
        cost_estimate=pl.CostEstimate(flops=0, bytes_accessed=moved, transcendentals=0),
    )(*given, *arrays)


PERMUTES = (
    (dict(dz=1), 2, (0, 16)),
    (dict(dx=1), 1, (0, 10)),
    (dict(dx=-1), -1, (0, 10)),
    (dict(dy=1), 1, (10, 16)),
    (dict(dy=-1), -1, (10, 16)),
)
BATCHES = ((1, 3), (2, 4), (0,))


def gather_slab(send, rows, block):
    shape = (CLASSES, CORES, COLOURS, rows, block)
    own = lax.all_to_all(send, AXES, 0, 0, axis_index_groups=exchange_groups())
    arrived = [fetch(own[lo:hi], **where) for where, _, (lo, hi) in PERMUTES]
    whole = None
    for at, batch in enumerate(BATCHES):
        parts = [(own, 0, (0, CLASSES))] if at == 0 else []
        parts += [(arrived[i], *PERMUTES[i][1:]) for i in batch]
        joined = jnp.concatenate([part[0] for part in parts], axis=0) if len(parts) > 1 else parts[0][0]
        there = fetch(joined, dcore=1)
        for array, other in ((joined, False), (there, True)):
            pieces, first = [], 0
            for _, offset, (lo, hi) in parts:
                pieces.append((array, first, hi - lo, lo, other, offset))
                first += hi - lo
            whole = put(whole, pieces, shape, send.dtype)
    return whole


def per_device(pseudo_grad, error_buf, momentum, params, picks):
    blocks, block = params.shape
    replicas = lax.axis_size("rep")
    own_picks = picks[0].astype(jnp.float32)
    topk = own_picks.shape[0]
    positions = lax.iota(jnp.float32, blocks)
    accumulated = DECAY_RATE * error_buf[0] + pseudo_grad[0]
    selector = (own_picks[:, None] == positions[None, :]).astype(jnp.float32)
    chosen_values = jnp.dot(selector, accumulated, precision=lax.Precision.HIGHEST)
    payload = jnp.concatenate(
        [chosen_values, jnp.broadcast_to(own_picks[:, None], (topk, LANES))], axis=1
    )
    everyone = lax.all_to_all(
        jnp.broadcast_to(payload[None], (replicas, topk, block + LANES)), "rep", 0, 0
    ).reshape(replicas * topk, block + LANES)
    new_params, new_momentum, send = update(everyone, momentum, params)
    gathered = gather_slab(send, blocks // COLOURS, block)
    chosen_mask = jnp.sum(selector, axis=0)
    new_error = (accumulated * (1.0 - chosen_mask)[:, None])[None]
    return (new_params, new_momentum, new_error, gathered.reshape(-1, block))


def solution(mesh):
    in_specs = (
        P("rep", "fsdp", None),
        P("rep", "fsdp", None),
        P("fsdp", None),
        P("fsdp", None),
        P("rep", "fsdp"),
    )
    out_specs = (P("fsdp", None), P("fsdp", None), P("rep", "fsdp", None), P())
    return jax.shard_map(
        per_device, mesh=mesh, in_specs=in_specs, out_specs=out_specs, check_vma=False
    )
```

```python
import jax
import jax.numpy as jnp
from jax import lax
from jax.experimental import pallas as pl
from jax.experimental.pallas import tpu as pltpu
from jax.sharding import PartitionSpec as P

DECAY_RATE = 0.95
MOMENTUM_COEF = 0.9
STEP_SCALE = 0.7
LANES = 128
AXES = ("rep", "fsdp")
NX, NY, NZ, CORES = 4, 8, 8, 2
CLASSES = 2 * NZ
COLOURS = 4
VMEM_LIMIT = 40 * 1024 * 1024


def device_at(x, y, z, core):
    x, y, z, core = x % NX, y % NY, z % NZ, core % CORES
    return (y * 2 + x % 2) * (2 * NZ * CORES) + (x // 2) * (NZ * CORES) + z * CORES + core


PLACES = [
    (x, y, z, core) for x in range(NX) for y in range(NY) for z in range(NZ) for core in range(CORES)
]


def fetch(value, dx=0, dy=0, dz=0, dcore=0):
    pairs = [
        (device_at(x + dx, y + dy, z + dz, core + dcore), device_at(x, y, z, core))
        for x, y, z, core in PLACES
    ]
    return lax.ppermute(value, AXES, pairs)


def exchange_groups():
    groups = []
    for x in range(NX // 2):
        for y in range(NY):
            for core in range(CORES):
                pair = sorted((x, NX - 1 - x), key=lambda v: v // 2)
                groups.append([device_at(v, y, z, core) for v in pair for z in range(NZ)])
    return groups


def place_of_self():
    rep, shard = lax.axis_index("rep"), lax.axis_index("fsdp")
    x = (shard // (NZ * CORES)) * 2 + rep % 2
    return x, rep // 2, (shard // CORES) % NZ, shard % CORES


def colour_of(x, y, z):
    return (x + y + 2 * z) % COLOURS


def choose_kernel(picks, error, grad, momentum, params, payload, momentum_near, params_near, rows, sems):
    topk, block = payload.shape[1], error.shape[1]
    loads = []
    for at in range(topk):
        first = pl.multiple_of((picks[at] // 8) * 8, 8)
        for which, array in enumerate((error, grad)):
            slot = 2 * at + which
            loads.append(
                pltpu.make_async_copy(array.at[pl.ds(first, 8)], rows.at[slot], sems.at[slot])
            )
    staged = [
        pltpu.make_async_copy(momentum, momentum_near, sems.at[2 * topk]),
        pltpu.make_async_copy(params, params_near, sems.at[2 * topk + 1]),
    ]
    for copy in loads + staged:
        copy.start()
    row_of = lax.broadcasted_iota(jnp.int32, (8, block), 0)
    pick_row = lax.broadcasted_iota(jnp.int32, (topk, LANES), 0)
    values = jnp.zeros((topk, block), jnp.float32)
    names = jnp.zeros((topk, LANES), jnp.float32)
    for copy in loads:
        copy.wait()
    for at in range(topk):
        group = DECAY_RATE * rows[2 * at] + rows[2 * at + 1]
        one = jnp.sum(jnp.where(row_of == picks[at] % 8, group, 0.0), axis=0, keepdims=True)
        values = jnp.where(row_of == at, one, values)
        names = jnp.where(pick_row == at, picks[at].astype(jnp.float32), names)
    for replica in range(payload.shape[0]):
        payload[replica, :, :block] = values
        payload[replica, :, block:] = names
    for copy in staged:
        copy.wait()


def choose(picks, error, grad, momentum, params, replicas):
    blocks, block = params.shape
    topk = picks.shape[0]
    vmem = pl.BlockSpec(memory_space=pltpu.VMEM)
    hbm = pl.BlockSpec(memory_space=pltpu.HBM)
    error, grad, momentum, params = (
        pltpu.with_memory_space_constraint(array, pltpu.HBM) for array in (error, grad, momentum, params)
    )
    return pl.pallas_call(
        choose_kernel,
        out_shape=(
            jax.ShapeDtypeStruct((replicas, topk, block + LANES), jnp.float32),
            jax.ShapeDtypeStruct((blocks, block), jnp.float32),
            jax.ShapeDtypeStruct((blocks, block), jnp.float32),
        ),
        in_specs=[pl.BlockSpec(memory_space=pltpu.SMEM)] + [hbm] * 4,
        out_specs=(vmem,) * 3,
        scratch_shapes=[
            pltpu.VMEM((2 * topk, 8, block), jnp.float32),
            pltpu.SemaphoreType.DMA((2 * topk + 2,)),
        ],
        compiler_params=pltpu.CompilerParams(vmem_limit_bytes=VMEM_LIMIT),
        cost_estimate=pl.CostEstimate(flops=10**5, bytes_accessed=2 * 10**6, transcendentals=0),
    )(picks, error, grad, momentum, params)


def update_kernel(everyone, momentum, params, new_params, new_momentum, send, shard):
    blocks, block = params.shape
    entries = everyone.shape[0]
    values = everyone[:, :block]
    picks = everyone[:, block:]
    lane = lax.broadcasted_iota(jnp.int32, (entries, LANES), 1).astype(jnp.float32)
    spread = jnp.concatenate(
        [(picks == lane + float(at)).astype(jnp.bfloat16) for at in range(0, blocks, LANES)], axis=1
    )
    delta = jnp.zeros((blocks, block), jnp.float32)
    rest = values
    for _ in range(3):
        part = rest.astype(jnp.bfloat16)
        rest = rest - part.astype(jnp.float32)
        delta += lax.dot_general(
            spread, part, (((0,), (0,)), ((), ())), preferred_element_type=jnp.float32
        )
    delta = delta / 16.0
    momentum_now = MOMENTUM_COEF * momentum[...] + delta
    params_now = params[...] - STEP_SCALE * (delta + MOMENTUM_COEF * momentum_now)
    new_momentum[...] = momentum_now
    new_params[...] = params_now
    shard[...] = params_now.astype(jnp.bfloat16)
    x, y, z, core = place_of_self()
    rows = blocks // COLOURS
    for x_hi in range(2):
        x_there = lax.select(x // 2 == x_hi, x, NX - 1 - x)
        for z_there in range(NZ):
            start = pl.multiple_of(colour_of(x_there, y, z_there) * rows, rows)
            send[x_hi * NZ + z_there] = shard[pl.ds(start, rows), :]


def update(everyone, momentum, params):
    blocks, block = params.shape
    vmem = pl.BlockSpec(memory_space=pltpu.VMEM)
    return pl.pallas_call(
        update_kernel,
        out_shape=(
            jax.ShapeDtypeStruct((blocks, block), jnp.float32),
            jax.ShapeDtypeStruct((blocks, block), jnp.float32),
            jax.ShapeDtypeStruct((CLASSES, blocks // COLOURS, block), jnp.bfloat16),
        ),
        in_specs=[vmem] * 3,
        out_specs=(vmem,) * 3,
        scratch_shapes=[pltpu.VMEM((blocks, block), jnp.bfloat16)],
        compiler_params=pltpu.CompilerParams(vmem_limit_bytes=VMEM_LIMIT),
        cost_estimate=pl.CostEstimate(flops=10**8, bytes_accessed=4 * 10**6, transcendentals=0),
    )(everyone, momentum, params)


def put(whole, pieces, shape, dtype):
    arrays = []
    for piece in pieces:
        if not any(piece[0] is a for a in arrays):
            arrays.append(piece[0])
    slots = [next(i for i, a in enumerate(arrays) if a is piece[0]) for piece in pieces]
    given = [] if whole is None else [whole]

    def kernel(*refs):
        sources = refs[len(given) : len(given) + len(arrays)]
        out, sems = refs[-2:]
        x, y, z, core = place_of_self()
        copies = []
        for piece, slot in zip(pieces, slots):
            _, first, count, cls, other, offset = piece
            there = 1 - core if other else core
            colour = (colour_of(x, y, z) + offset) % COLOURS
            for at in range(count):
                copies.append(
                    pltpu.make_async_copy(
                        sources[slot].at[first + at],
                        out.at[cls + at, there, colour],
                        sems.at[len(copies)],
                    )
                )
        for copy in copies:
            copy.start()
        for copy in copies:
            copy.wait()

    total = sum(piece[2] for piece in pieces)
    moved = 4 * total * pieces[0][0][0].size
    return pl.pallas_call(
        kernel,
        out_shape=jax.ShapeDtypeStruct(shape, dtype),
        in_specs=[pl.BlockSpec(memory_space=pltpu.HBM)] * len(given)
        + [pl.BlockSpec(memory_space=pltpu.VMEM)] * len(arrays),
        out_specs=pl.BlockSpec(memory_space=pltpu.HBM),
        scratch_shapes=[pltpu.SemaphoreType.DMA((total,))],
        input_output_aliases={0: 0} if given else {},
        compiler_params=pltpu.CompilerParams(vmem_limit_bytes=VMEM_LIMIT),
        cost_estimate=pl.CostEstimate(flops=0, bytes_accessed=moved, transcendentals=0),
    )(*given, *arrays)


PERMUTES = (
    (dict(dz=1), 2, (0, 16)),
    (dict(dx=1), 1, (0, 10)),
    (dict(dx=-1), -1, (0, 10)),
    (dict(dy=1), 1, (10, 16)),
    (dict(dy=-1), -1, (10, 16)),
)
BATCHES = ((1, 3, 2, 4), (0,))


def gather_slab(send, rows, block):
    shape = (CLASSES, CORES, COLOURS, rows, block)
    own = lax.all_to_all(send, AXES, 0, 0, axis_index_groups=exchange_groups())
    arrived = [fetch(own[lo:hi], **where) for where, _, (lo, hi) in PERMUTES]
    own_there = fetch(own, dcore=1)
    whole = put(None, [(own, 0, CLASSES, 0, False, 0)], shape, send.dtype)
    whole = put(whole, [(own_there, 0, CLASSES, 0, True, 0)], shape, send.dtype)
    *arrived, whole = lax.optimization_barrier((*arrived, whole))
    here, there = [], []
    for batch in BATCHES:
        parts = [(arrived[i], *PERMUTES[i][1:]) for i in batch]
        joined = jnp.concatenate([part[0] for part in parts], axis=0) if len(parts) > 1 else parts[0][0]
        for array, other, pieces in ((joined, False, here), (fetch(joined, dcore=1), True, there)):
            batch_pieces, first = [], 0
            for _, offset, (lo, hi) in parts:
                batch_pieces.append((array, first, hi - lo, lo, other, offset))
                first += hi - lo
            pieces.append(batch_pieces)
    for batch_pieces in here + there:
        whole = put(whole, batch_pieces, shape, send.dtype)
    return whole


def per_device(pseudo_grad, error_buf, momentum, params, picks):
    blocks, block = params.shape
    replicas = lax.axis_size("rep")
    own_picks = picks[0]
    payload, momentum_near, params_near = choose(
        own_picks, error_buf[0], pseudo_grad[0], momentum, params, replicas
    )
    everyone = lax.all_to_all(payload, "rep", 0, 0).reshape(-1, payload.shape[-1])
    new_params, new_momentum, send = update(everyone, momentum_near, params_near)
    gathered = gather_slab(send, blocks // COLOURS, block)
    accumulated = DECAY_RATE * error_buf[0] + pseudo_grad[0]
    chosen = jnp.any(own_picks[:, None] == lax.iota(jnp.int32, blocks)[None, :], axis=0)
    new_error = jnp.where(chosen[:, None], 0.0, accumulated)[None]
    return (new_params, new_momentum, new_error, gathered.reshape(-1, block))


def solution(mesh):
    in_specs = (
        P("rep", "fsdp", None),
        P("rep", "fsdp", None),
        P("fsdp", None),
        P("fsdp", None),
        P("rep", "fsdp"),
    )
    out_specs = (P("fsdp", None), P("fsdp", None), P("rep", "fsdp", None), P())
    return jax.shard_map(
        per_device, mesh=mesh, in_specs=in_specs, out_specs=out_specs, check_vma=False
    )
```

```python
import jax
import jax.numpy as jnp
from jax import lax
from jax.experimental import pallas as pl
from jax.experimental.pallas import tpu as pltpu
from jax.sharding import PartitionSpec as P

DECAY_RATE = 0.95
MOMENTUM_COEF = 0.9
STEP_SCALE = 0.7
LANES = 128
AXES = ("rep", "fsdp")
NX, NY, NZ, CORES = 4, 8, 8, 2
CLASSES = 2 * NZ
COLOURS = 8
SHIFTS = (1, 3)
VMEM_LIMIT = 40 * 1024 * 1024


def device_at(x, y, z, core):
    x, y, z, core = x % NX, y % NY, z % NZ, core % CORES
    return (y * 2 + x % 2) * (2 * NZ * CORES) + (x // 2) * (NZ * CORES) + z * CORES + core


PLACES = [
    (x, y, z, core) for x in range(NX) for y in range(NY) for z in range(NZ) for core in range(CORES)
]


def fetch(value, dx=0, dy=0, dz=0, dcore=0):
    pairs = [
        (device_at(x + dx, y + dy, z + dz, core + dcore), device_at(x, y, z, core))
        for x, y, z, core in PLACES
    ]
    return lax.ppermute(value, AXES, pairs)


def collect(shard, partner):
    pairs = []
    for x, y, z, core in PLACES:
        x_there = NX - 1 - x if partner else x
        z_there = colour_of(x, y, z) + SHIFTS[x_there // 2]
        pairs.append((device_at(x_there, y, z_there, core), device_at(x, y, z, core)))
    return lax.ppermute(shard, AXES, pairs)


def place_of_self():
    rep, shard = lax.axis_index("rep"), lax.axis_index("fsdp")
    x = (shard // (NZ * CORES)) * 2 + rep % 2
    return x, rep // 2, (shard // CORES) % NZ, shard % CORES


def colour_of(x, y, z):
    return (2 * x + y + 5 * z) % COLOURS


def choose_kernel(picks, error, grad, momentum, params, payload, momentum_near, params_near, rows, sems):
    topk, block = payload.shape[1], error.shape[1]
    loads = []
    for at in range(topk):
        first = pl.multiple_of((picks[at] // 8) * 8, 8)
        for which, array in enumerate((error, grad)):
            slot = 2 * at + which
            loads.append(
                pltpu.make_async_copy(array.at[pl.ds(first, 8)], rows.at[slot], sems.at[slot])
            )
    staged = [
        pltpu.make_async_copy(momentum, momentum_near, sems.at[2 * topk]),
        pltpu.make_async_copy(params, params_near, sems.at[2 * topk + 1]),
    ]
    for copy in loads + staged:
        copy.start()
    row_of = lax.broadcasted_iota(jnp.int32, (8, block), 0)
    pick_row = lax.broadcasted_iota(jnp.int32, (topk, LANES), 0)
    values = jnp.zeros((topk, block), jnp.float32)
    names = jnp.zeros((topk, LANES), jnp.float32)
    for copy in loads:
        copy.wait()
    for at in range(topk):
        group = DECAY_RATE * rows[2 * at] + rows[2 * at + 1]
        one = jnp.sum(jnp.where(row_of == picks[at] % 8, group, 0.0), axis=0, keepdims=True)
        values = jnp.where(row_of == at, one, values)
        names = jnp.where(pick_row == at, picks[at].astype(jnp.float32), names)
    for replica in range(payload.shape[0]):
        payload[replica, :, :block] = values
        payload[replica, :, block:] = names
    for copy in staged:
        copy.wait()


def choose(picks, error, grad, momentum, params, replicas):
    blocks, block = params.shape
    topk = picks.shape[0]
    vmem = pl.BlockSpec(memory_space=pltpu.VMEM)
    hbm = pl.BlockSpec(memory_space=pltpu.HBM)
    error, grad, momentum, params = (
        pltpu.with_memory_space_constraint(array, pltpu.HBM) for array in (error, grad, momentum, params)
    )
    return pl.pallas_call(
        choose_kernel,
        out_shape=(
            jax.ShapeDtypeStruct((replicas, topk, block + LANES), jnp.float32),
            jax.ShapeDtypeStruct((blocks, block), jnp.float32),
            jax.ShapeDtypeStruct((blocks, block), jnp.float32),
        ),
        in_specs=[pl.BlockSpec(memory_space=pltpu.SMEM)] + [hbm] * 4,
        out_specs=(vmem,) * 3,
        scratch_shapes=[
            pltpu.VMEM((2 * topk, 8, block), jnp.float32),
            pltpu.SemaphoreType.DMA((2 * topk + 2,)),
        ],
        compiler_params=pltpu.CompilerParams(vmem_limit_bytes=VMEM_LIMIT),
        cost_estimate=pl.CostEstimate(flops=10**5, bytes_accessed=2 * 10**6, transcendentals=0),
    )(picks, error, grad, momentum, params)


def update_kernel(everyone, momentum, params, new_params, new_momentum, shard):
    blocks, block = params.shape
    entries = everyone.shape[0]
    values = everyone[:, :block]
    picks = everyone[:, block:]
    lane = lax.broadcasted_iota(jnp.int32, (entries, LANES), 1).astype(jnp.float32)
    spread = jnp.concatenate(
        [(picks == lane + float(at)).astype(jnp.bfloat16) for at in range(0, blocks, LANES)], axis=1
    )
    delta = jnp.zeros((blocks, block), jnp.float32)
    rest = values
    for _ in range(3):
        part = rest.astype(jnp.bfloat16)
        rest = rest - part.astype(jnp.float32)
        delta += lax.dot_general(
            spread, part, (((0,), (0,)), ((), ())), preferred_element_type=jnp.float32
        )
    delta = delta / 16.0
    momentum_now = MOMENTUM_COEF * momentum[...] + delta
    params_now = params[...] - STEP_SCALE * (delta + MOMENTUM_COEF * momentum_now)
    new_momentum[...] = momentum_now
    new_params[...] = params_now
    shard[...] = params_now.astype(jnp.bfloat16)


def update(everyone, momentum, params):
    blocks, block = params.shape
    vmem = pl.BlockSpec(memory_space=pltpu.VMEM)
    return pl.pallas_call(
        update_kernel,
        out_shape=(
            jax.ShapeDtypeStruct((blocks, block), jnp.float32),
            jax.ShapeDtypeStruct((blocks, block), jnp.float32),
            jax.ShapeDtypeStruct((blocks, block), jnp.bfloat16),
        ),
        in_specs=[vmem] * 3,
        out_specs=(vmem,) * 3,
        compiler_params=pltpu.CompilerParams(vmem_limit_bytes=VMEM_LIMIT),
        cost_estimate=pl.CostEstimate(flops=10**8, bytes_accessed=4 * 10**6, transcendentals=0),
    )(everyone, momentum, params)


def put(whole, pieces, shape, dtype):
    arrays = []
    for piece in pieces:
        if not any(piece[0] is a for a in arrays):
            arrays.append(piece[0])
    slots = [next(i for i, a in enumerate(arrays) if a is piece[0]) for piece in pieces]
    given = [] if whole is None else [whole]

    def kernel(*refs):
        sources = refs[len(given) : len(given) + len(arrays)]
        out, sems = refs[-2:]
        x, y, z, core = place_of_self()
        copies = []
        for (_, first, offset, other), slot in zip(pieces, slots):
            x_there = (x + offset.get("dx", 0) + NX) % NX
            y_there = y + offset.get("dy", 0) + NY
            z_there = z + offset.get("dz", 0) + NZ
            colour = colour_of(x_there, y_there, z_there)
            own = x_there // 2
            for at, x_hi in enumerate((own, 1 - own)):
                shift = SHIFTS[0] + (SHIFTS[1] - SHIFTS[0]) * x_hi
                copies.append(
                    pltpu.make_async_copy(
                        sources[slot].at[first + at],
                        out.at[x_hi * NZ + (colour + shift) % NZ, 1 - core if other else core],
                        sems.at[len(copies)],
                    )
                )
        for copy in copies:
            copy.start()
        for copy in copies:
            copy.wait()

    total = 2 * len(pieces)
    return pl.pallas_call(
        kernel,
        out_shape=jax.ShapeDtypeStruct(shape, dtype),
        in_specs=[pl.BlockSpec(memory_space=pltpu.HBM)] * len(given)
        + [pl.BlockSpec(memory_space=pltpu.VMEM)] * len(arrays),
        out_specs=pl.BlockSpec(memory_space=pltpu.HBM),
        scratch_shapes=[pltpu.SemaphoreType.DMA((total,))],
        input_output_aliases={0: 0} if given else {},
        compiler_params=pltpu.CompilerParams(vmem_limit_bytes=VMEM_LIMIT),
        cost_estimate=pl.CostEstimate(
            flops=0, bytes_accessed=4 * total * shape[2] * shape[3], transcendentals=0
        ),
    )(*given, *arrays)


OTHERS = (
    dict(dy=1, dz=-1),
    dict(dx=1),
    dict(dx=-1),
    dict(dy=-1),
    dict(dz=1),
    dict(dy=1),
    dict(dz=-1),
)
BATCHES = ((0, 1, 2, 3), (4, 5, 6))


def gather_slab(shard):
    shape = (CLASSES, CORES, *shard.shape)
    portion = jnp.stack([collect(shard, partner=False), collect(shard, partner=True)])
    arrived = [fetch(portion, **offset) for offset in OTHERS]
    portion_there = fetch(portion, dcore=1)
    whole = put(None, [(portion, 0, {}, False)], shape, shard.dtype)
    whole = put(whole, [(portion_there, 0, {}, True)], shape, shard.dtype)
    *arrived, whole = lax.optimization_barrier((*arrived, whole))
    here, there = [], []
    for batch in BATCHES:
        joined = jnp.concatenate([arrived[i] for i in batch], axis=0)
        joined_there = fetch(joined, dcore=1)
        here.append([(joined, 2 * at, OTHERS[i], False) for at, i in enumerate(batch)])
        there.append([(joined_there, 2 * at, OTHERS[i], True) for at, i in enumerate(batch)])
    for pieces in here + there:
        whole = put(whole, pieces, shape, shard.dtype)
    return whole


def per_device(pseudo_grad, error_buf, momentum, params, picks):
    blocks, block = params.shape
    replicas = lax.axis_size("rep")
    own_picks = picks[0]
    payload, momentum_near, params_near = choose(
        own_picks, error_buf[0], pseudo_grad[0], momentum, params, replicas
    )
    everyone = lax.all_to_all(payload, "rep", 0, 0).reshape(-1, payload.shape[-1])
    new_params, new_momentum, shard = update(everyone, momentum_near, params_near)
    gathered = gather_slab(shard)
    accumulated = DECAY_RATE * error_buf[0] + pseudo_grad[0]
    chosen = jnp.any(own_picks[:, None] == lax.iota(jnp.int32, blocks)[None, :], axis=0)
    new_error = jnp.where(chosen[:, None], 0.0, accumulated)[None]
    return (new_params, new_momentum, new_error, gathered.reshape(-1, block))


def solution(mesh):
    in_specs = (
        P("rep", "fsdp", None),
        P("rep", "fsdp", None),
        P("fsdp", None),
        P("fsdp", None),
        P("rep", "fsdp"),
    )
    out_specs = (P("fsdp", None), P("fsdp", None), P("rep", "fsdp", None), P())
    return jax.shard_map(
        per_device, mesh=mesh, in_specs=in_specs, out_specs=out_specs, check_vma=False
    )
```

```python
import jax
import jax.numpy as jnp
from jax import lax
from jax.experimental import pallas as pl
from jax.experimental.pallas import tpu as pltpu
from jax.sharding import PartitionSpec as P

DECAY_RATE = 0.95
MOMENTUM_COEF = 0.9
STEP_SCALE = 0.7
LANES = 128
AXES = ("rep", "fsdp")
NX, NY, NZ, CORES = 4, 8, 8, 2
CLASSES = 2 * NZ
COLOURS = 8
SHIFTS = (1, 3)
VMEM_LIMIT = 40 * 1024 * 1024


def device_at(x, y, z, core):
    x, y, z, core = x % NX, y % NY, z % NZ, core % CORES
    return (y * 2 + x % 2) * (2 * NZ * CORES) + (x // 2) * (NZ * CORES) + z * CORES + core


PLACES = [
    (x, y, z, core) for x in range(NX) for y in range(NY) for z in range(NZ) for core in range(CORES)
]


def fetch(value, offsets):
    pairs = []
    for x, y, z, core in PLACES:
        dx, dy, dz = offsets[core]
        pairs.append((device_at(x + dx, y + dy, z + dz, core), device_at(x, y, z, core)))
    return lax.ppermute(value, AXES, pairs)


def swap(value):
    pairs = [(device_at(x, y, z, 1 - core), device_at(x, y, z, core)) for x, y, z, core in PLACES]
    return lax.ppermute(value, AXES, pairs)


def collect(shard, partner):
    pairs = []
    for x, y, z, core in PLACES:
        x_there = NX - 1 - x if partner else x
        z_there = colour_of(x, y, z) + SHIFTS[x_there // 2]
        pairs.append((device_at(x_there, y, z_there, core), device_at(x, y, z, core)))
    return lax.ppermute(shard, AXES, pairs)


def place_of_self():
    rep, shard = lax.axis_index("rep"), lax.axis_index("fsdp")
    x = (shard // (NZ * CORES)) * 2 + rep % 2
    return x, rep // 2, (shard // CORES) % NZ, shard % CORES


def colour_of(x, y, z):
    return (2 * x + y + 5 * z) % COLOURS


def choose_kernel(picks, error, grad, momentum, params, payload, momentum_near, params_near, rows, sems):
    topk, block = payload.shape[1], error.shape[1]
    loads = []
    for at in range(topk):
        first = pl.multiple_of((picks[at] // 8) * 8, 8)
        for which, array in enumerate((error, grad)):
            slot = 2 * at + which
            loads.append(
                pltpu.make_async_copy(array.at[pl.ds(first, 8)], rows.at[slot], sems.at[slot])
            )
    staged = [
        pltpu.make_async_copy(momentum, momentum_near, sems.at[2 * topk]),
        pltpu.make_async_copy(params, params_near, sems.at[2 * topk + 1]),
    ]
    for copy in loads + staged:
        copy.start()
    row_of = lax.broadcasted_iota(jnp.int32, (8, block), 0)
    pick_row = lax.broadcasted_iota(jnp.int32, (topk, LANES), 0)
    values = jnp.zeros((topk, block), jnp.float32)
    names = jnp.zeros((topk, LANES), jnp.float32)
    for copy in loads:
        copy.wait()
    for at in range(topk):
        group = DECAY_RATE * rows[2 * at] + rows[2 * at + 1]
        one = jnp.sum(jnp.where(row_of == picks[at] % 8, group, 0.0), axis=0, keepdims=True)
        values = jnp.where(row_of == at, one, values)
        names = jnp.where(pick_row == at, picks[at].astype(jnp.float32), names)
    for replica in range(payload.shape[0]):
        payload[replica, :, :block] = values
        payload[replica, :, block:] = names
    for copy in staged:
        copy.wait()


def choose(picks, error, grad, momentum, params, replicas):
    blocks, block = params.shape
    topk = picks.shape[0]
    vmem = pl.BlockSpec(memory_space=pltpu.VMEM)
    hbm = pl.BlockSpec(memory_space=pltpu.HBM)
    error, grad, momentum, params = (
        pltpu.with_memory_space_constraint(array, pltpu.HBM) for array in (error, grad, momentum, params)
    )
    return pl.pallas_call(
        choose_kernel,
        out_shape=(
            jax.ShapeDtypeStruct((replicas, topk, block + LANES), jnp.float32),
            jax.ShapeDtypeStruct((blocks, block), jnp.float32),
            jax.ShapeDtypeStruct((blocks, block), jnp.float32),
        ),
        in_specs=[pl.BlockSpec(memory_space=pltpu.SMEM)] + [hbm] * 4,
        out_specs=(vmem,) * 3,
        scratch_shapes=[
            pltpu.VMEM((2 * topk, 8, block), jnp.float32),
            pltpu.SemaphoreType.DMA((2 * topk + 2,)),
        ],
        compiler_params=pltpu.CompilerParams(vmem_limit_bytes=VMEM_LIMIT),
        cost_estimate=pl.CostEstimate(flops=10**5, bytes_accessed=2 * 10**6, transcendentals=0),
    )(picks, error, grad, momentum, params)


def update_kernel(everyone, momentum, params, new_params, new_momentum, shard):
    blocks, block = params.shape
    entries = everyone.shape[0]
    values = everyone[:, :block]
    picks = everyone[:, block:]
    lane = lax.broadcasted_iota(jnp.int32, (entries, LANES), 1).astype(jnp.float32)
    spread = jnp.concatenate(
        [(picks == lane + float(at)).astype(jnp.bfloat16) for at in range(0, blocks, LANES)], axis=1
    )
    delta = jnp.zeros((blocks, block), jnp.float32)
    rest = values
    for _ in range(3):
        part = rest.astype(jnp.bfloat16)
        rest = rest - part.astype(jnp.float32)
        delta += lax.dot_general(
            spread, part, (((0,), (0,)), ((), ())), preferred_element_type=jnp.float32
        )
    delta = delta / 16.0
    momentum_now = MOMENTUM_COEF * momentum[...] + delta
    params_now = params[...] - STEP_SCALE * (delta + MOMENTUM_COEF * momentum_now)
    new_momentum[...] = momentum_now
    new_params[...] = params_now
    shard[...] = params_now.astype(jnp.bfloat16)


def update(everyone, momentum, params):
    blocks, block = params.shape
    vmem = pl.BlockSpec(memory_space=pltpu.VMEM)
    return pl.pallas_call(
        update_kernel,
        out_shape=(
            jax.ShapeDtypeStruct((blocks, block), jnp.float32),
            jax.ShapeDtypeStruct((blocks, block), jnp.float32),
            jax.ShapeDtypeStruct((blocks, block), jnp.bfloat16),
        ),
        in_specs=[vmem] * 3,
        out_specs=(vmem,) * 3,
        compiler_params=pltpu.CompilerParams(vmem_limit_bytes=VMEM_LIMIT),
        cost_estimate=pl.CostEstimate(flops=10**8, bytes_accessed=4 * 10**6, transcendentals=0),
    )(everyone, momentum, params)


def put(whole, pieces, shape, dtype):
    arrays = []
    for piece in pieces:
        if not any(piece[0] is a for a in arrays):
            arrays.append(piece[0])
    slots = [next(i for i, a in enumerate(arrays) if a is piece[0]) for piece in pieces]
    given = [] if whole is None else [whole]

    def kernel(*refs):
        sources = refs[len(given) : len(given) + len(arrays)]
        out, sems = refs[-2:]
        x, y, z, core = place_of_self()
        copies = []
        for (_, first, count, offsets, other), slot in zip(pieces, slots):
            by = 1 - core if other else core
            dx, dy, dz = (one + (two - one) * by for one, two in zip(*offsets))
            x_there = (x + dx + NX) % NX
            colour = colour_of(x_there, y + dy + NY, z + dz + NZ)
            own = x_there // 2
            for at in range(count):
                x_hi = 1 - own if at % 2 else own
                shift = SHIFTS[0] + (SHIFTS[1] - SHIFTS[0]) * x_hi
                copies.append(
                    pltpu.make_async_copy(
                        sources[slot].at[first + at],
                        out.at[x_hi * NZ + (colour + shift) % NZ, 1 - by if at >= 2 else by],
                        sems.at[len(copies)],
                    )
                )
        for copy in copies:
            copy.start()
        for copy in copies:
            copy.wait()

    total = sum(piece[2] for piece in pieces)
    return pl.pallas_call(
        kernel,
        out_shape=jax.ShapeDtypeStruct(shape, dtype),
        in_specs=[pl.BlockSpec(memory_space=pltpu.HBM)] * len(given)
        + [pl.BlockSpec(memory_space=pltpu.VMEM)] * len(arrays),
        out_specs=pl.BlockSpec(memory_space=pltpu.HBM),
        scratch_shapes=[pltpu.SemaphoreType.DMA((total,))],
        input_output_aliases={0: 0} if given else {},
        compiler_params=pltpu.CompilerParams(vmem_limit_bytes=VMEM_LIMIT),
        cost_estimate=pl.CostEstimate(
            flops=0, bytes_accessed=4 * total * shape[2] * shape[3], transcendentals=0
        ),
    )(*given, *arrays)


HERE = ((0, 0, 0), (0, 0, 0))
OPPOSITE = ((0, 1, -1), (0, -1, 1))
NEIGHBOURS = (
    ((1, 0, 0), (-1, 0, 0)),
    ((0, 1, 0), (0, -1, 0)),
    ((0, 0, 1), (0, 0, -1)),
)


def gather_slab(shard):
    shape = (CLASSES, CORES, *shard.shape)
    half = jnp.stack([collect(shard, partner=False), collect(shard, partner=True)])
    opposite = fetch(half, OPPOSITE)
    portion = jnp.concatenate([half, swap(half)], axis=0)
    arrived = [fetch(portion, offsets) for offsets in NEIGHBOURS]
    whole = put(None, [(portion, 0, 4, HERE, False)], shape, shard.dtype)
    opposite, *arrived, whole = lax.optimization_barrier((opposite, *arrived, whole))
    batches = (
        ((arrived[0], 4, NEIGHBOURS[0]), (arrived[1], 4, NEIGHBOURS[1])),
        ((arrived[2], 4, NEIGHBOURS[2]), (opposite, 2, OPPOSITE)),
    )
    here, there = [], []
    for batch in batches:
        joined = jnp.concatenate([array for array, _, _ in batch], axis=0)
        joined_there = swap(joined)
        firsts = (0, batch[0][1])
        here.append([(joined, at, n, off, False) for at, (_, n, off) in zip(firsts, batch)])
        there.append([(joined_there, at, n, off, True) for at, (_, n, off) in zip(firsts, batch)])
    for pieces in here + there:
        whole = put(whole, pieces, shape, shard.dtype)
    return whole


def per_device(pseudo_grad, error_buf, momentum, params, picks):
    blocks, block = params.shape
    replicas = lax.axis_size("rep")
    own_picks = picks[0]
    payload, momentum_near, params_near = choose(
        own_picks, error_buf[0], pseudo_grad[0], momentum, params, replicas
    )
    everyone = lax.all_to_all(payload, "rep", 0, 0).reshape(-1, payload.shape[-1])
    new_params, new_momentum, shard = update(everyone, momentum_near, params_near)
    gathered = gather_slab(shard)
    accumulated = DECAY_RATE * error_buf[0] + pseudo_grad[0]
    chosen = jnp.any(own_picks[:, None] == lax.iota(jnp.int32, blocks)[None, :], axis=0)
    new_error = jnp.where(chosen[:, None], 0.0, accumulated)[None]
    return (new_params, new_momentum, new_error, gathered.reshape(-1, block))


def solution(mesh):
    in_specs = (
        P("rep", "fsdp", None),
        P("rep", "fsdp", None),
        P("fsdp", None),
        P("fsdp", None),
        P("rep", "fsdp"),
    )
    out_specs = (P("fsdp", None), P("fsdp", None), P("rep", "fsdp", None), P())
    return jax.shard_map(
        per_device, mesh=mesh, in_specs=in_specs, out_specs=out_specs, check_vma=False
    )
```

```python
import jax
import jax.numpy as jnp
from jax import lax
from jax.experimental import pallas as pl
from jax.experimental.pallas import tpu as pltpu
from jax.sharding import PartitionSpec as P

DECAY_RATE = 0.95
MOMENTUM_COEF = 0.9
STEP_SCALE = 0.7
LANES = 128
AXES = ("rep", "fsdp")
NX, NY, NZ, CORES = 4, 8, 8, 2
CLASSES = 2 * NZ
COLOURS = 8
SHIFTS = (1, 3)
VMEM_LIMIT = 40 * 1024 * 1024


def device_at(x, y, z, core):
    x, y, z, core = x % NX, y % NY, z % NZ, core % CORES
    return (y * 2 + x % 2) * (2 * NZ * CORES) + (x // 2) * (NZ * CORES) + z * CORES + core


PLACES = [
    (x, y, z, core) for x in range(NX) for y in range(NY) for z in range(NZ) for core in range(CORES)
]


def fetch(value, offsets):
    pairs = []
    for x, y, z, core in PLACES:
        dx, dy, dz = offsets[core]
        pairs.append((device_at(x + dx, y + dy, z + dz, core), device_at(x, y, z, core)))
    return lax.ppermute(value, AXES, pairs)


def swap(value):
    pairs = [(device_at(x, y, z, 1 - core), device_at(x, y, z, core)) for x, y, z, core in PLACES]
    return lax.ppermute(value, AXES, pairs)


def collect(shard, partner):
    pairs = []
    for x, y, z, core in PLACES:
        x_there = NX - 1 - x if partner else x
        z_there = colour_of(x, y, z) + SHIFTS[x_there // 2]
        pairs.append((device_at(x_there, y, z_there, core), device_at(x, y, z, core)))
    return lax.ppermute(shard, AXES, pairs)


def place_of_self():
    rep, shard = lax.axis_index("rep"), lax.axis_index("fsdp")
    x = (shard // (NZ * CORES)) * 2 + rep % 2
    return x, rep // 2, (shard // CORES) % NZ, shard % CORES


def colour_of(x, y, z):
    return (2 * x + y + 5 * z) % COLOURS


def choose_kernel(
    picks_hbm, error, grad, momentum, params, payload, momentum_near, params_near, picks_smem, rows, sems
):
    topk, block = payload.shape[1], error.shape[1]
    staged = [
        pltpu.make_async_copy(momentum, momentum_near, sems.at[2 * topk]),
        pltpu.make_async_copy(params, params_near, sems.at[2 * topk + 1]),
    ]
    names_load = pltpu.make_async_copy(picks_hbm, picks_smem, sems.at[2 * topk + 2])
    names_load.start()
    for copy in staged:
        copy.start()
    names_load.wait()
    picks = [picks_smem[0, at] for at in range(topk)]
    loads = []
    for at in range(topk):
        first = pl.multiple_of((picks[at] // 8) * 8, 8)
        for which, array in enumerate((error, grad)):
            slot = 2 * at + which
            loads.append(
                pltpu.make_async_copy(array.at[pl.ds(first, 8)], rows.at[slot], sems.at[slot])
            )
    for copy in loads:
        copy.start()
    row_of = lax.broadcasted_iota(jnp.int32, (8, block), 0)
    pick_row = lax.broadcasted_iota(jnp.int32, (topk, LANES), 0)
    values = jnp.zeros((topk, block), jnp.float32)
    names = jnp.zeros((topk, LANES), jnp.float32)
    for copy in loads:
        copy.wait()
    for at in range(topk):
        group = DECAY_RATE * rows[2 * at] + rows[2 * at + 1]
        one = jnp.sum(jnp.where(row_of == picks[at] % 8, group, 0.0), axis=0, keepdims=True)
        values = jnp.where(row_of == at, one, values)
        names = jnp.where(pick_row == at, picks[at].astype(jnp.float32), names)
    for replica in range(payload.shape[0]):
        payload[replica, :, :block] = values
        payload[replica, :, block:] = names
    for copy in staged:
        copy.wait()


def choose(picks, error, grad, momentum, params, replicas):
    blocks, block = params.shape
    topk = picks.shape[1]
    vmem = pl.BlockSpec(memory_space=pltpu.VMEM)
    hbm = pl.BlockSpec(memory_space=pltpu.HBM)
    picks, error, grad, momentum, params = (
        pltpu.with_memory_space_constraint(array, pltpu.HBM)
        for array in (picks, error, grad, momentum, params)
    )
    return pl.pallas_call(
        choose_kernel,
        out_shape=(
            jax.ShapeDtypeStruct((replicas, topk, block + LANES), jnp.float32),
            jax.ShapeDtypeStruct((blocks, block), jnp.float32),
            jax.ShapeDtypeStruct((blocks, block), jnp.float32),
        ),
        in_specs=[hbm] * 5,
        out_specs=(vmem,) * 3,
        scratch_shapes=[
            pltpu.SMEM((1, topk), jnp.int32),
            pltpu.VMEM((2 * topk, 8, block), jnp.float32),
            pltpu.SemaphoreType.DMA((2 * topk + 3,)),
        ],
        compiler_params=pltpu.CompilerParams(vmem_limit_bytes=VMEM_LIMIT),
        cost_estimate=pl.CostEstimate(flops=10**5, bytes_accessed=2 * 10**6, transcendentals=0),
    )(picks, error, grad, momentum, params)


def update_kernel(everyone, momentum, params, new_params, new_momentum, shard):
    blocks, block = params.shape
    entries = everyone.shape[0]
    values = everyone[:, :block]
    picks = everyone[:, block:]
    lane = lax.broadcasted_iota(jnp.int32, (entries, LANES), 1).astype(jnp.float32)
    spread = jnp.concatenate(
        [(picks == lane + float(at)).astype(jnp.bfloat16) for at in range(0, blocks, LANES)], axis=1
    )
    delta = jnp.zeros((blocks, block), jnp.float32)
    rest = values
    for _ in range(3):
        part = rest.astype(jnp.bfloat16)
        rest = rest - part.astype(jnp.float32)
        delta += lax.dot_general(
            spread, part, (((0,), (0,)), ((), ())), preferred_element_type=jnp.float32
        )
    delta = delta / 16.0
    momentum_now = MOMENTUM_COEF * momentum[...] + delta
    params_now = params[...] - STEP_SCALE * (delta + MOMENTUM_COEF * momentum_now)
    new_momentum[...] = momentum_now
    new_params[...] = params_now
    shard[...] = params_now.astype(jnp.bfloat16)


def update(everyone, momentum, params):
    blocks, block = params.shape
    vmem = pl.BlockSpec(memory_space=pltpu.VMEM)
    return pl.pallas_call(
        update_kernel,
        out_shape=(
            jax.ShapeDtypeStruct((blocks, block), jnp.float32),
            jax.ShapeDtypeStruct((blocks, block), jnp.float32),
            jax.ShapeDtypeStruct((blocks, block), jnp.bfloat16),
        ),
        in_specs=[vmem] * 3,
        out_specs=(vmem,) * 3,
        compiler_params=pltpu.CompilerParams(vmem_limit_bytes=VMEM_LIMIT),
        cost_estimate=pl.CostEstimate(flops=10**8, bytes_accessed=4 * 10**6, transcendentals=0),
    )(everyone, momentum, params)


def put(whole, pieces, shape, dtype):
    arrays = []
    for piece in pieces:
        if not any(piece[0] is a for a in arrays):
            arrays.append(piece[0])
    slots = [next(i for i, a in enumerate(arrays) if a is piece[0]) for piece in pieces]
    given = [] if whole is None else [whole]

    def kernel(*refs):
        sources = refs[len(given) : len(given) + len(arrays)]
        out, sems = refs[-2:]
        x, y, z, core = place_of_self()
        copies = []
        for (_, first, count, place, offsets, other), slot in zip(pieces, slots):
            by = 1 - core if other else core
            dx, dy, dz = (one + (two - one) * by for one, two in zip(*offsets))
            x_there = (x + dx + NX) % NX
            colour = colour_of(x_there, y + dy + NY, z + dz + NZ)
            own = x_there // 2
            for at in range(count):
                x_hi = 1 - own if (place + at) % 2 else own
                shift = SHIFTS[0] + (SHIFTS[1] - SHIFTS[0]) * x_hi
                copies.append(
                    pltpu.make_async_copy(
                        sources[slot].at[first + at],
                        out.at[x_hi * NZ + (colour + shift) % NZ, 1 - by if place + at >= 2 else by],
                        sems.at[len(copies)],
                    )
                )
        for copy in copies:
            copy.start()
        for copy in copies:
            copy.wait()

    total = sum(piece[2] for piece in pieces)
    return pl.pallas_call(
        kernel,
        out_shape=jax.ShapeDtypeStruct(shape, dtype),
        in_specs=[pl.BlockSpec(memory_space=pltpu.HBM)] * len(given)
        + [pl.BlockSpec(memory_space=pltpu.VMEM)] * len(arrays),
        out_specs=pl.BlockSpec(memory_space=pltpu.HBM),
        scratch_shapes=[pltpu.SemaphoreType.DMA((total,))],
        input_output_aliases={0: 0} if given else {},
        compiler_params=pltpu.CompilerParams(vmem_limit_bytes=VMEM_LIMIT),
        cost_estimate=pl.CostEstimate(
            flops=0, bytes_accessed=4 * total * shape[2] * shape[3], transcendentals=0
        ),
    )(*given, *arrays)


HERE = ((0, 0, 0), (0, 0, 0))
OPPOSITE = ((0, 1, -1), (0, -1, 1))
NEIGHBOURS = (
    ((0, 1, 0), (0, -1, 0)),
    ((0, 0, 1), (0, 0, -1)),
    ((1, 0, 0), (-1, 0, 0)),
)


def gather_slab(shard, aside):
    shape = (CLASSES, CORES, *shard.shape)
    half = jnp.stack([collect(shard, partner=False), collect(shard, partner=True)])
    opposite = fetch(half, OPPOSITE)
    portion = jnp.concatenate([half, swap(half)], axis=0)
    near_y, near_z, near_x = (fetch(portion, offsets) for offsets in NEIGHBOURS)
    whole = put(None, [(portion, 0, 4, 0, HERE, False)], shape, shard.dtype)
    pieces = [(near_y, 0, 4, 0, NEIGHBOURS[0], False)]
    pieces += [(swap(near_y[at : at + 2]), 0, 2, at, NEIGHBOURS[0], True) for at in (0, 2)]
    whole = put(whole, pieces, shape, shard.dtype)
    near_z, near_x, opposite, whole, aside = lax.optimization_barrier(
        (near_z, near_x, opposite, whole, aside)
    )
    batches = (
        ((near_x, 4, NEIGHBOURS[2]), (opposite, 2, OPPOSITE)),
        ((near_z, 4, NEIGHBOURS[1]),),
    )
    here, there = [], []
    for batch in batches:
        joined = jnp.concatenate([array for array, _, _ in batch], axis=0)
        for array, other, placed in ((joined, False, here), (swap(joined), True, there)):
            firsts = (0, batch[0][1])
            placed.append([(array, at, n, 0, off, other) for at, (_, n, off) in zip(firsts, batch)])
    for pieces in (here[0] + here[1], *there):
        whole = put(whole, pieces, shape, shard.dtype)
    return whole, aside


def per_device(pseudo_grad, error_buf, momentum, params, picks):
    blocks, block = params.shape
    replicas = lax.axis_size("rep")
    own_picks = picks[0]
    payload, momentum_near, params_near = choose(
        picks, error_buf[0], pseudo_grad[0], momentum, params, replicas
    )
    everyone = lax.all_to_all(payload, "rep", 0, 0).reshape(-1, payload.shape[-1])
    new_params, new_momentum, shard = update(everyone, momentum_near, params_near)
    accumulated = DECAY_RATE * error_buf[0] + pseudo_grad[0]
    chosen = jnp.any(own_picks[:, None] == lax.iota(jnp.int32, blocks)[None, :], axis=0)
    new_error = jnp.where(chosen[:, None], 0.0, accumulated)[None]
    gathered, new_error = gather_slab(shard, new_error)
    return (new_params, new_momentum, new_error, gathered.reshape(-1, block))


def solution(mesh):
    in_specs = (
        P("rep", "fsdp", None),
        P("rep", "fsdp", None),
        P("fsdp", None),
        P("fsdp", None),
        P("rep", "fsdp"),
    )
    out_specs = (P("fsdp", None), P("fsdp", None), P("rep", "fsdp", None), P())
    return jax.shard_map(
        per_device, mesh=mesh, in_specs=in_specs, out_specs=out_specs, check_vma=False
    )
```

```python
import jax
import jax.numpy as jnp
from jax import lax
from jax.experimental import pallas as pl
from jax.experimental.pallas import tpu as pltpu
from jax.sharding import PartitionSpec as P

DECAY_RATE = 0.95
MOMENTUM_COEF = 0.9
STEP_SCALE = 0.7
LANES = 128
AXES = ("rep", "fsdp")
NX, NY, NZ, CORES = 4, 8, 8, 2
CLASSES = 2 * NZ
COLOURS = 8
SHIFTS = (1, 3)
VMEM_LIMIT = 40 * 1024 * 1024


def device_at(x, y, z, core):
    x, y, z, core = x % NX, y % NY, z % NZ, core % CORES
    return (y * 2 + x % 2) * (2 * NZ * CORES) + (x // 2) * (NZ * CORES) + z * CORES + core


PLACES = [
    (x, y, z, core) for x in range(NX) for y in range(NY) for z in range(NZ) for core in range(CORES)
]


def fetch(value, offsets):
    pairs = []
    for x, y, z, core in PLACES:
        dx, dy, dz = offsets[core]
        pairs.append((device_at(x + dx, y + dy, z + dz, core), device_at(x, y, z, core)))
    return lax.ppermute(value, AXES, pairs)


def swap(value):
    pairs = [(device_at(x, y, z, 1 - core), device_at(x, y, z, core)) for x, y, z, core in PLACES]
    return lax.ppermute(value, AXES, pairs)


def collect(shard, partner):
    pairs = []
    for x, y, z, core in PLACES:
        x_there = NX - 1 - x if partner else x
        z_there = colour_of(x, y, z) + SHIFTS[x_there // 2]
        pairs.append((device_at(x_there, y, z_there, core), device_at(x, y, z, core)))
    return lax.ppermute(shard, AXES, pairs)


def place_of_self():
    rep, shard = lax.axis_index("rep"), lax.axis_index("fsdp")
    x = (shard // (NZ * CORES)) * 2 + rep % 2
    return x, rep // 2, (shard // CORES) % NZ, shard % CORES


def colour_of(x, y, z):
    return (2 * x + y + 5 * z) % COLOURS


def choose_kernel(
    picks_hbm, error, grad, momentum, params, payload, momentum_near, params_near, picks_smem, rows, sems
):
    topk, block = payload.shape[1], error.shape[1]
    staged = [
        pltpu.make_async_copy(momentum, momentum_near, sems.at[2 * topk]),
        pltpu.make_async_copy(params, params_near, sems.at[2 * topk + 1]),
    ]
    names_load = pltpu.make_async_copy(picks_hbm, picks_smem, sems.at[2 * topk + 2])
    names_load.start()
    for copy in staged:
        copy.start()
    names_load.wait()
    picks = [picks_smem[0, at] for at in range(topk)]
    loads = []
    for at in range(topk):
        first = pl.multiple_of((picks[at] // 8) * 8, 8)
        for which, array in enumerate((error, grad)):
            slot = 2 * at + which
            loads.append(
                pltpu.make_async_copy(array.at[pl.ds(first, 8)], rows.at[slot], sems.at[slot])
            )
    for copy in loads:
        copy.start()
    row_of = lax.broadcasted_iota(jnp.int32, (8, block), 0)
    pick_row = lax.broadcasted_iota(jnp.int32, (topk, LANES), 0)
    values = jnp.zeros((topk, block), jnp.float32)
    names = jnp.zeros((topk, LANES), jnp.float32)
    for copy in loads:
        copy.wait()
    for at in range(topk):
        group = DECAY_RATE * rows[2 * at] + rows[2 * at + 1]
        one = jnp.sum(jnp.where(row_of == picks[at] % 8, group, 0.0), axis=0, keepdims=True)
        values = jnp.where(row_of == at, one, values)
        names = jnp.where(pick_row == at, picks[at].astype(jnp.float32), names)
    for replica in range(payload.shape[0]):
        payload[replica, :, :block] = values
        payload[replica, :, block:] = names
    for copy in staged:
        copy.wait()


def choose(picks, error, grad, momentum, params, replicas):
    blocks, block = params.shape
    topk = picks.shape[1]
    vmem = pl.BlockSpec(memory_space=pltpu.VMEM)
    hbm = pl.BlockSpec(memory_space=pltpu.HBM)
    picks, error, grad, momentum, params = (
        pltpu.with_memory_space_constraint(array, pltpu.HBM)
        for array in (picks, error, grad, momentum, params)
    )
    return pl.pallas_call(
        choose_kernel,
        out_shape=(
            jax.ShapeDtypeStruct((replicas, topk, block + LANES), jnp.float32),
            jax.ShapeDtypeStruct((blocks, block), jnp.float32),
            jax.ShapeDtypeStruct((blocks, block), jnp.float32),
        ),
        in_specs=[hbm] * 5,
        out_specs=(vmem,) * 3,
        scratch_shapes=[
            pltpu.SMEM((1, topk), jnp.int32),
            pltpu.VMEM((2 * topk, 8, block), jnp.float32),
            pltpu.SemaphoreType.DMA((2 * topk + 3,)),
        ],
        compiler_params=pltpu.CompilerParams(vmem_limit_bytes=VMEM_LIMIT),
        cost_estimate=pl.CostEstimate(flops=10**5, bytes_accessed=2 * 10**6, transcendentals=0),
    )(picks, error, grad, momentum, params)


def update_kernel(everyone, momentum, params, new_params, new_momentum, shard):
    blocks, block = params.shape
    entries = everyone.shape[0]
    values = everyone[:, :block]
    picks = everyone[:, block:]
    lane = lax.broadcasted_iota(jnp.int32, (entries, LANES), 1).astype(jnp.float32)
    spread = jnp.concatenate(
        [(picks == lane + float(at)).astype(jnp.bfloat16) for at in range(0, blocks, LANES)], axis=1
    )
    delta = jnp.zeros((blocks, block), jnp.float32)
    rest = values
    for _ in range(3):
        part = rest.astype(jnp.bfloat16)
        rest = rest - part.astype(jnp.float32)
        delta += lax.dot_general(
            spread, part, (((0,), (0,)), ((), ())), preferred_element_type=jnp.float32
        )
    delta = delta / 16.0
    momentum_now = MOMENTUM_COEF * momentum[...] + delta
    params_now = params[...] - STEP_SCALE * (delta + MOMENTUM_COEF * momentum_now)
    new_momentum[...] = momentum_now
    new_params[...] = params_now
    shard[...] = params_now.astype(jnp.bfloat16)


def update(everyone, momentum, params):
    blocks, block = params.shape
    vmem = pl.BlockSpec(memory_space=pltpu.VMEM)
    return pl.pallas_call(
        update_kernel,
        out_shape=(
            jax.ShapeDtypeStruct((blocks, block), jnp.float32),
            jax.ShapeDtypeStruct((blocks, block), jnp.float32),
            jax.ShapeDtypeStruct((blocks, block), jnp.bfloat16),
        ),
        in_specs=[vmem] * 3,
        out_specs=(vmem,) * 3,
        compiler_params=pltpu.CompilerParams(vmem_limit_bytes=VMEM_LIMIT),
        cost_estimate=pl.CostEstimate(flops=10**8, bytes_accessed=4 * 10**6, transcendentals=0),
    )(everyone, momentum, params)


def put(whole, pieces, shape, dtype):
    arrays = []
    for piece in pieces:
        if not any(piece[0] is a for a in arrays):
            arrays.append(piece[0])
    slots = [next(i for i, a in enumerate(arrays) if a is piece[0]) for piece in pieces]
    given = [] if whole is None else [whole]

    def kernel(*refs):
        sources = refs[len(given) : len(given) + len(arrays)]
        out, sems = refs[-2:]
        x, y, z, core = place_of_self()
        copies = []
        for (_, first, count, place, offsets, other), slot in zip(pieces, slots):
            by = 1 - core if other else core
            dx, dy, dz = (one + (two - one) * by for one, two in zip(*offsets))
            x_there = (x + dx + NX) % NX
            colour = colour_of(x_there, y + dy + NY, z + dz + NZ)
            own = x_there // 2
            for at in range(count):
                x_hi = 1 - own if (place + at) % 2 else own
                shift = SHIFTS[0] + (SHIFTS[1] - SHIFTS[0]) * x_hi
                copies.append(
                    pltpu.make_async_copy(
                        sources[slot].at[first + at],
                        out.at[x_hi * NZ + (colour + shift) % NZ, 1 - by if place + at >= 2 else by],
                        sems.at[len(copies)],
                    )
                )
        for copy in copies:
            copy.start()
        for copy in copies:
            copy.wait()

    total = sum(piece[2] for piece in pieces)
    return pl.pallas_call(
        kernel,
        out_shape=jax.ShapeDtypeStruct(shape, dtype),
        in_specs=[pl.BlockSpec(memory_space=pltpu.HBM)] * len(given)
        + [pl.BlockSpec(memory_space=pltpu.VMEM)] * len(arrays),
        out_specs=pl.BlockSpec(memory_space=pltpu.HBM),
        scratch_shapes=[pltpu.SemaphoreType.DMA((total,))],
        input_output_aliases={0: 0} if given else {},
        compiler_params=pltpu.CompilerParams(vmem_limit_bytes=VMEM_LIMIT),
        cost_estimate=pl.CostEstimate(
            flops=0, bytes_accessed=4 * total * shape[2] * shape[3], transcendentals=0
        ),
    )(*given, *arrays)


HERE = ((0, 0, 0), (0, 0, 0))
OPPOSITE = ((0, 1, -1), (0, -1, 1))
NEIGHBOURS = (
    ((0, 1, 0), (0, -1, 0)),
    ((0, 0, 1), (0, 0, -1)),
    ((1, 0, 0), (-1, 0, 0)),
)


def gather_slab(shard, aside):
    shape = (CLASSES, CORES, *shard.shape)
    half = jnp.stack([collect(shard, partner=False), collect(shard, partner=True)])
    opposite = fetch(half, OPPOSITE)
    portion = jnp.concatenate([half, swap(half)], axis=0)
    near_y, near_z, near_x = (fetch(portion, offsets) for offsets in NEIGHBOURS)
    whole = put(None, [(portion, 0, 4, 0, HERE, False)], shape, shard.dtype)
    pieces = [(near_y, 0, 4, 0, NEIGHBOURS[0], False), (opposite, 0, 2, 0, OPPOSITE, False)]
    pieces += [(swap(near_y[at : at + 2]), 0, 2, at, NEIGHBOURS[0], True) for at in (0, 2)]
    pieces += [(swap(opposite), 0, 2, 0, OPPOSITE, True)]
    whole = put(whole, pieces, shape, shard.dtype)
    near_z, near_x, whole, aside = lax.optimization_barrier((near_z, near_x, whole, aside))
    batches = ((near_z, NEIGHBOURS[1]), (near_x, NEIGHBOURS[2]))
    here = [(array, 0, 4, 0, offsets, False) for array, offsets in batches]
    there = [(swap(array), 0, 4, 0, offsets, True) for array, offsets in batches]
    for pieces in (here, there[:1], there[1:]):
        whole = put(whole, pieces, shape, shard.dtype)
    return whole, aside


def per_device(pseudo_grad, error_buf, momentum, params, picks):
    blocks, block = params.shape
    replicas = lax.axis_size("rep")
    own_picks = picks[0]
    payload, momentum_near, params_near = choose(
        picks, error_buf[0], pseudo_grad[0], momentum, params, replicas
    )
    everyone = lax.all_to_all(payload, "rep", 0, 0).reshape(-1, payload.shape[-1])
    new_params, new_momentum, shard = update(everyone, momentum_near, params_near)
    accumulated = DECAY_RATE * error_buf[0] + pseudo_grad[0]
    chosen = jnp.any(own_picks[:, None] == lax.iota(jnp.int32, blocks)[None, :], axis=0)
    new_error = jnp.where(chosen[:, None], 0.0, accumulated)[None]
    gathered, new_error = gather_slab(shard, new_error)
    return (new_params, new_momentum, new_error, gathered.reshape(-1, block))


def solution(mesh):
    in_specs = (
        P("rep", "fsdp", None),
        P("rep", "fsdp", None),
        P("fsdp", None),
        P("fsdp", None),
        P("rep", "fsdp"),
    )
    out_specs = (P("fsdp", None), P("fsdp", None), P("rep", "fsdp", None), P())
    return jax.shard_map(
        per_device, mesh=mesh, in_specs=in_specs, out_specs=out_specs, check_vma=False
    )
```

```python
import jax
import jax.numpy as jnp
from jax import lax
from jax.experimental import pallas as pl
from jax.experimental.pallas import tpu as pltpu
from jax.sharding import PartitionSpec as P

DECAY_RATE = 0.95
MOMENTUM_COEF = 0.9
STEP_SCALE = 0.7
LANES = 128
AXES = ("rep", "fsdp")
NX, NY, NZ, CORES = 4, 8, 8, 2
CLASSES = 2 * NZ
COLOURS = 8
SHIFTS = (1, 3)
VMEM_LIMIT = 40 * 1024 * 1024


def device_at(x, y, z, core):
    x, y, z, core = x % NX, y % NY, z % NZ, core % CORES
    return (y * 2 + x % 2) * (2 * NZ * CORES) + (x // 2) * (NZ * CORES) + z * CORES + core


PLACES = [
    (x, y, z, core) for x in range(NX) for y in range(NY) for z in range(NZ) for core in range(CORES)
]


def fetch(value, offsets):
    pairs = []
    for x, y, z, core in PLACES:
        dx, dy, dz = offsets[core]
        pairs.append((device_at(x + dx, y + dy, z + dz, core), device_at(x, y, z, core)))
    return lax.ppermute(value, AXES, pairs)


def swap(value):
    pairs = [(device_at(x, y, z, 1 - core), device_at(x, y, z, core)) for x, y, z, core in PLACES]
    return lax.ppermute(value, AXES, pairs)


def collect(shard, partner):
    pairs = []
    for x, y, z, core in PLACES:
        x_there = NX - 1 - x if partner else x
        z_there = colour_of(x, y, z) + SHIFTS[x_there // 2]
        pairs.append((device_at(x_there, y, z_there, core), device_at(x, y, z, core)))
    return lax.ppermute(shard, AXES, pairs)


def place_of_self():
    rep, shard = lax.axis_index("rep"), lax.axis_index("fsdp")
    x = (shard // (NZ * CORES)) * 2 + rep % 2
    return x, rep // 2, (shard // CORES) % NZ, shard % CORES


def colour_of(x, y, z):
    return (2 * x + y + 5 * z) % COLOURS


def choose_kernel(
    picks_hbm, error, grad, momentum, params, payload, momentum_near, params_near, picks_smem, rows, sems
):
    topk, block = payload.shape[1], error.shape[1]
    staged = [
        pltpu.make_async_copy(momentum, momentum_near, sems.at[2 * topk]),
        pltpu.make_async_copy(params, params_near, sems.at[2 * topk + 1]),
    ]
    names_load = pltpu.make_async_copy(picks_hbm, picks_smem, sems.at[2 * topk + 2])
    names_load.start()
    for copy in staged:
        copy.start()
    names_load.wait()
    picks = [picks_smem[0, at] for at in range(topk)]
    loads = []
    for at in range(topk):
        first = pl.multiple_of((picks[at] // 8) * 8, 8)
        for which, array in enumerate((error, grad)):
            slot = 2 * at + which
            loads.append(
                pltpu.make_async_copy(array.at[pl.ds(first, 8)], rows.at[slot], sems.at[slot])
            )
    for copy in loads:
        copy.start()
    row_of = lax.broadcasted_iota(jnp.int32, (8, block), 0)
    pick_row = lax.broadcasted_iota(jnp.int32, (topk, LANES), 0)
    values = jnp.zeros((topk, block), jnp.float32)
    names = jnp.zeros((topk, LANES), jnp.float32)
    for copy in loads:
        copy.wait()
    for at in range(topk):
        group = DECAY_RATE * rows[2 * at] + rows[2 * at + 1]
        one = jnp.sum(jnp.where(row_of == picks[at] % 8, group, 0.0), axis=0, keepdims=True)
        values = jnp.where(row_of == at, one, values)
        names = jnp.where(pick_row == at, picks[at].astype(jnp.float32), names)
    for replica in range(payload.shape[0]):
        payload[replica, :, :block] = values
        payload[replica, :, block:] = names
    for copy in staged:
        copy.wait()


def choose(picks, error, grad, momentum, params, replicas):
    blocks, block = params.shape
    topk = picks.shape[1]
    vmem = pl.BlockSpec(memory_space=pltpu.VMEM)
    hbm = pl.BlockSpec(memory_space=pltpu.HBM)
    picks, error, grad, momentum, params = (
        pltpu.with_memory_space_constraint(array, pltpu.HBM)
        for array in (picks, error, grad, momentum, params)
    )
    return pl.pallas_call(
        choose_kernel,
        out_shape=(
            jax.ShapeDtypeStruct((replicas, topk, block + LANES), jnp.float32),
            jax.ShapeDtypeStruct((blocks, block), jnp.float32),
            jax.ShapeDtypeStruct((blocks, block), jnp.float32),
        ),
        in_specs=[hbm] * 5,
        out_specs=(vmem,) * 3,
        scratch_shapes=[
            pltpu.SMEM((1, topk), jnp.int32),
            pltpu.VMEM((2 * topk, 8, block), jnp.float32),
            pltpu.SemaphoreType.DMA((2 * topk + 3,)),
        ],
        compiler_params=pltpu.CompilerParams(vmem_limit_bytes=VMEM_LIMIT),
        cost_estimate=pl.CostEstimate(flops=10**5, bytes_accessed=2 * 10**6, transcendentals=0),
    )(picks, error, grad, momentum, params)


def update_kernel(everyone, momentum, params, new_params, new_momentum, shard):
    blocks, block = params.shape
    entries = everyone.shape[0]
    values = everyone[:, :block]
    picks = everyone[:, block:]
    lane = lax.broadcasted_iota(jnp.int32, (entries, LANES), 1).astype(jnp.float32)
    spread = jnp.concatenate(
        [(picks == lane + float(at)).astype(jnp.bfloat16) for at in range(0, blocks, LANES)], axis=1
    )
    delta = jnp.zeros((blocks, block), jnp.float32)
    rest = values
    for _ in range(3):
        part = rest.astype(jnp.bfloat16)
        rest = rest - part.astype(jnp.float32)
        delta += lax.dot_general(
            spread, part, (((0,), (0,)), ((), ())), preferred_element_type=jnp.float32
        )
    delta = delta / 16.0
    momentum_now = MOMENTUM_COEF * momentum[...] + delta
    params_now = params[...] - STEP_SCALE * (delta + MOMENTUM_COEF * momentum_now)
    new_momentum[...] = momentum_now
    new_params[...] = params_now
    shard[...] = params_now.astype(jnp.bfloat16)


def update(everyone, momentum, params):
    blocks, block = params.shape
    vmem = pl.BlockSpec(memory_space=pltpu.VMEM)
    return pl.pallas_call(
        update_kernel,
        out_shape=(
            jax.ShapeDtypeStruct((blocks, block), jnp.float32),
            jax.ShapeDtypeStruct((blocks, block), jnp.float32),
            jax.ShapeDtypeStruct((blocks, block), jnp.bfloat16),
        ),
        in_specs=[vmem] * 3,
        out_specs=(vmem,) * 3,
        compiler_params=pltpu.CompilerParams(vmem_limit_bytes=VMEM_LIMIT),
        cost_estimate=pl.CostEstimate(flops=10**8, bytes_accessed=4 * 10**6, transcendentals=0),
    )(everyone, momentum, params)


def put(whole, pieces, shape, dtype):
    arrays = []
    for piece in pieces:
        if not any(piece[0] is a for a in arrays):
            arrays.append(piece[0])
    slots = [next(i for i, a in enumerate(arrays) if a is piece[0]) for piece in pieces]
    given = [] if whole is None else [whole]

    def kernel(*refs):
        sources = refs[len(given) : len(given) + len(arrays)]
        out, sems = refs[-2:]
        x, y, z, core = place_of_self()
        copies = []
        for (_, first, count, place, offsets, other), slot in zip(pieces, slots):
            by = 1 - core if other else core
            dx, dy, dz = (one + (two - one) * by for one, two in zip(*offsets))
            x_there = (x + dx + NX) % NX
            colour = colour_of(x_there, y + dy + NY, z + dz + NZ)
            own = x_there // 2
            for at in range(count):
                x_hi = 1 - own if (place + at) % 2 else own
                shift = SHIFTS[0] + (SHIFTS[1] - SHIFTS[0]) * x_hi
                copies.append(
                    pltpu.make_async_copy(
                        sources[slot].at[first + at],
                        out.at[x_hi * NZ + (colour + shift) % NZ, 1 - by if place + at >= 2 else by],
                        sems.at[len(copies)],
                    )
                )
        for copy in copies:
            copy.start()
        for copy in copies:
            copy.wait()

    total = sum(piece[2] for piece in pieces)
    return pl.pallas_call(
        kernel,
        out_shape=jax.ShapeDtypeStruct(shape, dtype),
        in_specs=[pl.BlockSpec(memory_space=pltpu.HBM)] * len(given)
        + [pl.BlockSpec(memory_space=pltpu.VMEM)] * len(arrays),
        out_specs=pl.BlockSpec(memory_space=pltpu.HBM),
        scratch_shapes=[pltpu.SemaphoreType.DMA((total,))],
        input_output_aliases={0: 0} if given else {},
        compiler_params=pltpu.CompilerParams(vmem_limit_bytes=VMEM_LIMIT),
        cost_estimate=pl.CostEstimate(
            flops=0, bytes_accessed=4 * total * shape[2] * shape[3], transcendentals=0
        ),
    )(*given, *arrays)


HERE = ((0, 0, 0), (0, 0, 0))
X = ((1, 0, 0), (-1, 0, 0))
XX = ((2, 0, 0), (-2, 0, 0))
Y = ((0, 1, 0), (0, -1, 0))
Z = ((0, 0, 1), (0, 0, -1))


def gather_slab(shard, aside):
    shape = (CLASSES, CORES, *shard.shape)
    own, partners = collect(shard, partner=False), collect(shard, partner=True)
    own, partners, aside = lax.optimization_barrier((own, partners, aside))
    half = jnp.stack([own, partners])
    near_x = fetch(half, X)
    portion = jnp.concatenate([half, swap(half)], axis=0)
    near_y, near_z = fetch(portion, Y), fetch(portion, Z)
    far_x = fetch(jnp.concatenate(lax.optimization_barrier((portion[2:], near_x)), axis=0), X)
    whole = put(None, [(portion, 0, 4, 0, HERE, False)], shape, shard.dtype)
    pieces = [(near_x, 0, 2, 0, X, False)]
    for array, offsets in ((near_y, Y), (near_z, Z)):
        pieces += [(array, 0, 4, 0, offsets, False), (swap(array[:2]), 0, 2, 0, offsets, True)]
    whole = put(whole, pieces, shape, shard.dtype)
    near_x, near_y, near_z, far_x, whole = lax.optimization_barrier(
        (near_x, near_y, near_z, far_x, whole)
    )
    rest = swap(jnp.concatenate([near_x, near_y[2:], near_z[2:]], axis=0))
    far_there = swap(far_x)
    for pieces in (
        [(far_x, 0, 2, 2, X, False), (far_x, 2, 2, 0, XX, False)],
        [(rest, 0, 2, 0, X, True), (rest, 2, 2, 2, Y, True), (rest, 4, 2, 2, Z, True)],
        [(far_there, 0, 2, 2, X, True), (far_there, 2, 2, 0, XX, True)],
    ):
        whole = put(whole, pieces, shape, shard.dtype)
    return whole, aside


def per_device(pseudo_grad, error_buf, momentum, params, picks):
    blocks, block = params.shape
    replicas = lax.axis_size("rep")
    own_picks = picks[0]
    payload, momentum_near, params_near = choose(
        picks, error_buf[0], pseudo_grad[0], momentum, params, replicas
    )
    everyone = lax.all_to_all(payload, "rep", 0, 0).reshape(-1, payload.shape[-1])
    new_params, new_momentum, shard = update(everyone, momentum_near, params_near)
    accumulated = DECAY_RATE * error_buf[0] + pseudo_grad[0]
    chosen = jnp.any(own_picks[:, None] == lax.iota(jnp.int32, blocks)[None, :], axis=0)
    new_error = jnp.where(chosen[:, None], 0.0, accumulated)[None]
    gathered, new_error = gather_slab(shard, new_error)
    return (new_params, new_momentum, new_error, gathered.reshape(-1, block))


def solution(mesh):
    in_specs = (
        P("rep", "fsdp", None),
        P("rep", "fsdp", None),
        P("fsdp", None),
        P("fsdp", None),
        P("rep", "fsdp"),
    )
    out_specs = (P("fsdp", None), P("fsdp", None), P("rep", "fsdp", None), P())
    return jax.shard_map(
        per_device, mesh=mesh, in_specs=in_specs, out_specs=out_specs, check_vma=False
    )
```

```python
import jax
import jax.numpy as jnp
from jax import lax
from jax.experimental import pallas as pl
from jax.experimental.pallas import tpu as pltpu
from jax.sharding import PartitionSpec as P

DECAY_RATE = 0.95
MOMENTUM_COEF = 0.9
STEP_SCALE = 0.7
LANES = 128
AXES = ("rep", "fsdp")
NX, NY, NZ, CORES = 4, 8, 8, 2
CLASSES = 2 * NZ
COLOURS = 8
VMEM_LIMIT = 40 * 1024 * 1024


def z_of(colour, x_hi, core):
    return (colour + 1 + 4 * core - x_hi + NZ) % NZ


def device_at(x, y, z, core):
    x, y, z, core = x % NX, y % NY, z % NZ, core % CORES
    return (y * 2 + x % 2) * (2 * NZ * CORES) + (x // 2) * (NZ * CORES) + z * CORES + core


PLACES = [
    (x, y, z, core) for x in range(NX) for y in range(NY) for z in range(NZ) for core in range(CORES)
]


def fetch(value, offsets):
    pairs = []
    for x, y, z, core in PLACES:
        dx, dy, dz = offsets[core]
        pairs.append((device_at(x + dx, y + dy, z + dz, core), device_at(x, y, z, core)))
    return lax.ppermute(value, AXES, pairs)


def swap(value):
    pairs = [(device_at(x, y, z, 1 - core), device_at(x, y, z, core)) for x, y, z, core in PLACES]
    return lax.ppermute(value, AXES, pairs)


def collect(shard, partner):
    pairs = []
    for x, y, z, core in PLACES:
        x_there = NX - 1 - x if partner else x
        z_there = z_of(colour_of(x, y, z), x_there // 2, core)
        pairs.append((device_at(x_there, y, z_there, core), device_at(x, y, z, core)))
    return lax.ppermute(shard, AXES, pairs)


def place_of_self():
    rep, shard = lax.axis_index("rep"), lax.axis_index("fsdp")
    x = (shard // (NZ * CORES)) * 2 + rep % 2
    return x, rep // 2, (shard // CORES) % NZ, shard % CORES


def colour_of(x, y, z):
    return (2 * x + y + 3 * z) % COLOURS


def choose_kernel(
    picks_hbm, error, grad, momentum, params, payload, momentum_near, params_near, picks_smem, rows, sems
):
    topk, block = payload.shape[1], error.shape[1]
    staged = [
        pltpu.make_async_copy(momentum, momentum_near, sems.at[2 * topk]),
        pltpu.make_async_copy(params, params_near, sems.at[2 * topk + 1]),
    ]
    names_load = pltpu.make_async_copy(picks_hbm, picks_smem, sems.at[2 * topk + 2])
    names_load.start()
    for copy in staged:
        copy.start()
    names_load.wait()
    picks = [picks_smem[0, at] for at in range(topk)]
    loads = []
    for at in range(topk):
        first = pl.multiple_of((picks[at] // 8) * 8, 8)
        for which, array in enumerate((error, grad)):
            slot = 2 * at + which
            loads.append(
                pltpu.make_async_copy(array.at[pl.ds(first, 8)], rows.at[slot], sems.at[slot])
            )
    for copy in loads:
        copy.start()
    row_of = lax.broadcasted_iota(jnp.int32, (8, block), 0)
    pick_row = lax.broadcasted_iota(jnp.int32, (topk, LANES), 0)
    values = jnp.zeros((topk, block), jnp.float32)
    names = jnp.zeros((topk, LANES), jnp.float32)
    for copy in loads:
        copy.wait()
    for at in range(topk):
        group = DECAY_RATE * rows[2 * at] + rows[2 * at + 1]
        one = jnp.sum(jnp.where(row_of == picks[at] % 8, group, 0.0), axis=0, keepdims=True)
        values = jnp.where(row_of == at, one, values)
        names = jnp.where(pick_row == at, picks[at].astype(jnp.float32), names)
    for replica in range(payload.shape[0]):
        payload[replica, :, :block] = values
        payload[replica, :, block:] = names
    for copy in staged:
        copy.wait()


def choose(picks, error, grad, momentum, params, replicas):
    blocks, block = params.shape
    topk = picks.shape[1]
    vmem = pl.BlockSpec(memory_space=pltpu.VMEM)
    hbm = pl.BlockSpec(memory_space=pltpu.HBM)
    picks, error, grad, momentum, params = (
        pltpu.with_memory_space_constraint(array, pltpu.HBM)
        for array in (picks, error, grad, momentum, params)
    )
    return pl.pallas_call(
        choose_kernel,
        out_shape=(
            jax.ShapeDtypeStruct((replicas, topk, block + LANES), jnp.float32),
            jax.ShapeDtypeStruct((blocks, block), jnp.float32),
            jax.ShapeDtypeStruct((blocks, block), jnp.float32),
        ),
        in_specs=[hbm] * 5,
        out_specs=(vmem,) * 3,
        scratch_shapes=[
            pltpu.SMEM((1, topk), jnp.int32),
            pltpu.VMEM((2 * topk, 8, block), jnp.float32),
            pltpu.SemaphoreType.DMA((2 * topk + 3,)),
        ],
        compiler_params=pltpu.CompilerParams(vmem_limit_bytes=VMEM_LIMIT),
        cost_estimate=pl.CostEstimate(flops=10**5, bytes_accessed=2 * 10**6, transcendentals=0),
    )(picks, error, grad, momentum, params)


def keep_kernel(picks_hbm, error_hbm, grad_hbm, new_error, picks_smem, error, grad, sems):
    copies = [
        pltpu.make_async_copy(picks_hbm, picks_smem, sems.at[0]),
        pltpu.make_async_copy(error_hbm, error, sems.at[1]),
        pltpu.make_async_copy(grad_hbm, grad, sems.at[2]),
    ]
    for copy in copies:
        copy.start()
    for copy in copies:
        copy.wait()
    row = lax.broadcasted_iota(jnp.int32, error.shape, 0)
    chosen = row == picks_smem[0, 0]
    for at in range(1, picks_smem.shape[1]):
        chosen = chosen | (row == picks_smem[0, at])
    new_error[...] = jnp.where(chosen, 0.0, DECAY_RATE * error[...] + grad[...])


def keep(picks, error, grad):
    hbm = pl.BlockSpec(memory_space=pltpu.HBM)
    picks, error, grad = (
        pltpu.with_memory_space_constraint(array, pltpu.HBM) for array in (picks, error, grad)
    )
    return pl.pallas_call(
        keep_kernel,
        out_shape=jax.ShapeDtypeStruct(error.shape, jnp.float32),
        in_specs=[hbm] * 3,
        out_specs=pl.BlockSpec(memory_space=pltpu.VMEM),
        scratch_shapes=[
            pltpu.SMEM(picks.shape, jnp.int32),
            pltpu.VMEM(error.shape, jnp.float32),
            pltpu.VMEM(error.shape, jnp.float32),
            pltpu.SemaphoreType.DMA((3,)),
        ],
        compiler_params=pltpu.CompilerParams(vmem_limit_bytes=VMEM_LIMIT),
        cost_estimate=pl.CostEstimate(flops=10**6, bytes_accessed=2 * 10**6, transcendentals=0),
    )(picks, error, grad)


def update_kernel(everyone, momentum, params, new_params, new_momentum, shard):
    blocks, block = params.shape
    entries = everyone.shape[0]
    values = everyone[:, :block]
    picks = everyone[:, block:]
    lane = lax.broadcasted_iota(jnp.int32, (entries, LANES), 1).astype(jnp.float32)
    spread = jnp.concatenate(
        [(picks == lane + float(at)).astype(jnp.bfloat16) for at in range(0, blocks, LANES)], axis=1
    )
    delta = jnp.zeros((blocks, block), jnp.float32)
    rest = values
    for _ in range(3):
        part = rest.astype(jnp.bfloat16)
        rest = rest - part.astype(jnp.float32)
        delta += lax.dot_general(
            spread, part, (((0,), (0,)), ((), ())), preferred_element_type=jnp.float32
        )
    delta = delta / 16.0
    momentum_now = MOMENTUM_COEF * momentum[...] + delta
    params_now = params[...] - STEP_SCALE * (delta + MOMENTUM_COEF * momentum_now)
    new_momentum[...] = momentum_now
    new_params[...] = params_now
    shard[...] = params_now.astype(jnp.bfloat16)


def update(everyone, momentum, params):
    blocks, block = params.shape
    vmem = pl.BlockSpec(memory_space=pltpu.VMEM)
    return pl.pallas_call(
        update_kernel,
        out_shape=(
            jax.ShapeDtypeStruct((blocks, block), jnp.float32),
            jax.ShapeDtypeStruct((blocks, block), jnp.float32),
            jax.ShapeDtypeStruct((blocks, block), jnp.bfloat16),
        ),
        in_specs=[vmem] * 3,
        out_specs=(vmem,) * 3,
        compiler_params=pltpu.CompilerParams(vmem_limit_bytes=VMEM_LIMIT),
        cost_estimate=pl.CostEstimate(flops=10**8, bytes_accessed=4 * 10**6, transcendentals=0),
    )(everyone, momentum, params)


def put(whole, pieces, shape, dtype):
    arrays = []
    for piece in pieces:
        if not any(piece[0] is a for a in arrays):
            arrays.append(piece[0])
    slots = [next(i for i, a in enumerate(arrays) if a is piece[0]) for piece in pieces]
    given = [] if whole is None else [whole]

    def kernel(*refs):
        sources = refs[len(given) : len(given) + len(arrays)]
        out, sems = refs[-2:]
        x, y, z, core = place_of_self()
        copies = []
        for (_, first, count, place, offsets, other), slot in zip(pieces, slots):
            by = 1 - core if other else core
            dx, dy, dz = (one + (two - one) * by for one, two in zip(*offsets))
            x_there = (x + dx + NX) % NX
            colour = colour_of(x_there, y + dy + NY, z + dz + NZ)
            own = x_there // 2
            for at in range(count):
                x_hi = 1 - own if (place + at) % 2 else own
                from_core = 1 - by if place + at >= 2 else by
                copies.append(
                    pltpu.make_async_copy(
                        sources[slot].at[first + at],
                        out.at[x_hi * NZ + z_of(colour, x_hi, from_core), from_core],
                        sems.at[len(copies)],
                    )
                )
        for copy in copies:
            copy.start()
        for copy in copies:
            copy.wait()

    total = sum(piece[2] for piece in pieces)
    return pl.pallas_call(
        kernel,
        out_shape=jax.ShapeDtypeStruct(shape, dtype),
        in_specs=[pl.BlockSpec(memory_space=pltpu.HBM)] * len(given)
        + [pl.BlockSpec(memory_space=pltpu.VMEM)] * len(arrays),
        out_specs=pl.BlockSpec(memory_space=pltpu.HBM),
        scratch_shapes=[pltpu.SemaphoreType.DMA((total,))],
        input_output_aliases={0: 0} if given else {},
        compiler_params=pltpu.CompilerParams(vmem_limit_bytes=VMEM_LIMIT),
        cost_estimate=pl.CostEstimate(
            flops=0, bytes_accessed=4 * total * shape[2] * shape[3], transcendentals=0
        ),
    )(*given, *arrays)


HERE = ((0, 0, 0), (0, 0, 0))
X = ((1, 0, 0), (-1, 0, 0))
XX = ((2, 0, 0), (-2, 0, 0))
Y = ((0, 1, 0), (0, -1, 0))
Z = ((0, 0, 1), (0, 0, -1))


def gather_slab(shard, aside):
    shape = (CLASSES, CORES, *shard.shape)
    own, partners = collect(shard, partner=False), collect(shard, partner=True)
    own, partners, aside = lax.optimization_barrier((own, partners, aside))
    half = jnp.stack([own, partners])
    near_x = fetch(half, X)
    portion = jnp.concatenate([half, swap(half)], axis=0)
    near_y, near_z = fetch(portion, Y), fetch(portion, Z)
    far_x = fetch(jnp.concatenate(lax.optimization_barrier((portion[2:], near_x)), axis=0), X)
    whole = put(None, [(portion, 0, 4, 0, HERE, False)], shape, shard.dtype)
    pieces = [(near_x, 0, 2, 0, X, False)]
    for array, offsets in ((near_y, Y), (near_z, Z)):
        pieces += [(array, 0, 4, 0, offsets, False), (swap(array[:2]), 0, 2, 0, offsets, True)]
    whole = put(whole, pieces, shape, shard.dtype)
    near_x, near_y, near_z, far_x, whole = lax.optimization_barrier(
        (near_x, near_y, near_z, far_x, whole)
    )
    rest = swap(jnp.concatenate([near_x, near_y[2:], near_z[2:]], axis=0))
    far_there = swap(far_x)
    for pieces in (
        [(far_x, 0, 2, 2, X, False), (far_x, 2, 2, 0, XX, False)],
        [(rest, 0, 2, 0, X, True), (rest, 2, 2, 2, Y, True), (rest, 4, 2, 2, Z, True)],
        [(far_there, 0, 2, 2, X, True), (far_there, 2, 2, 0, XX, True)],
    ):
        whole = put(whole, pieces, shape, shard.dtype)
    return whole, aside


def per_device(pseudo_grad, error_buf, momentum, params, picks):
    blocks, block = params.shape
    replicas = lax.axis_size("rep")
    payload, momentum_near, params_near = choose(
        picks, error_buf[0], pseudo_grad[0], momentum, params, replicas
    )
    everyone = lax.all_to_all(payload, "rep", 0, 0).reshape(-1, payload.shape[-1])
    new_params, new_momentum, shard = update(everyone, momentum_near, params_near)
    error_buf, pseudo_grad, shard = lax.optimization_barrier((error_buf, pseudo_grad, shard))
    new_error = keep(picks, error_buf[0], pseudo_grad[0])[None]
    gathered, new_error = gather_slab(shard, new_error)
    return (new_params, new_momentum, new_error, gathered.reshape(-1, block))


def solution(mesh):
    in_specs = (
        P("rep", "fsdp", None),
        P("rep", "fsdp", None),
        P("fsdp", None),
        P("fsdp", None),
        P("rep", "fsdp"),
    )
    out_specs = (P("fsdp", None), P("fsdp", None), P("rep", "fsdp", None), P())
    return jax.shard_map(
        per_device, mesh=mesh, in_specs=in_specs, out_specs=out_specs, check_vma=False
    )
```

```python
import jax
import jax.numpy as jnp
from jax import lax
from jax.experimental import pallas as pl
from jax.experimental.pallas import tpu as pltpu
from jax.sharding import PartitionSpec as P

DECAY_RATE = 0.95
MOMENTUM_COEF = 0.9
STEP_SCALE = 0.7
LANES = 128
AXES = ("rep", "fsdp")
NX, NY, NZ, CORES = 4, 8, 8, 2
CLASSES = 2 * NZ
COLOURS = 8
VMEM_LIMIT = 40 * 1024 * 1024


def z_of(colour, x_hi, core):
    return (colour + 1 + 4 * core - x_hi + NZ) % NZ


def device_at(x, y, z, core):
    x, y, z, core = x % NX, y % NY, z % NZ, core % CORES
    return (y * 2 + x % 2) * (2 * NZ * CORES) + (x // 2) * (NZ * CORES) + z * CORES + core


PLACES = [
    (x, y, z, core) for x in range(NX) for y in range(NY) for z in range(NZ) for core in range(CORES)
]


def fetch(value, offsets):
    pairs = []
    for x, y, z, core in PLACES:
        dx, dy, dz = offsets[core]
        pairs.append((device_at(x + dx, y + dy, z + dz, core), device_at(x, y, z, core)))
    return lax.ppermute(value, AXES, pairs)


def swap(value):
    pairs = [(device_at(x, y, z, 1 - core), device_at(x, y, z, core)) for x, y, z, core in PLACES]
    return lax.ppermute(value, AXES, pairs)


def collect(shard, partner):
    pairs = []
    for x, y, z, core in PLACES:
        x_there = NX - 1 - x if partner else x
        z_there = z_of(colour_of(x, y, z), x_there // 2, core)
        pairs.append((device_at(x_there, y, z_there, core), device_at(x, y, z, core)))
    return lax.ppermute(shard, AXES, pairs)


def place_of_self():
    rep, shard = lax.axis_index("rep"), lax.axis_index("fsdp")
    x = (shard // (NZ * CORES)) * 2 + rep % 2
    return x, rep // 2, (shard // CORES) % NZ, shard % CORES


def colour_of(x, y, z):
    return (2 * x + y + 3 * z) % COLOURS


def choose_kernel(
    picks_hbm, error, grad, momentum, params, payload, momentum_near, params_near, picks_smem, rows, sems
):
    topk, block = payload.shape[1], error.shape[1]
    staged = [
        pltpu.make_async_copy(momentum, momentum_near, sems.at[2 * topk]),
        pltpu.make_async_copy(params, params_near, sems.at[2 * topk + 1]),
    ]
    names_load = pltpu.make_async_copy(picks_hbm, picks_smem, sems.at[2 * topk + 2])
    names_load.start()
    for copy in staged:
        copy.start()
    names_load.wait()
    picks = [picks_smem[0, at] for at in range(topk)]
    loads = []
    for at in range(topk):
        first = pl.multiple_of((picks[at] // 8) * 8, 8)
        for which, array in enumerate((error, grad)):
            slot = 2 * at + which
            loads.append(
                pltpu.make_async_copy(array.at[pl.ds(first, 8)], rows.at[slot], sems.at[slot])
            )
    for copy in loads:
        copy.start()
    row_of = lax.broadcasted_iota(jnp.int32, (8, block), 0)
    pick_row = lax.broadcasted_iota(jnp.int32, (topk, LANES), 0)
    values = jnp.zeros((topk, block), jnp.float32)
    names = jnp.zeros((topk, LANES), jnp.float32)
    for copy in loads:
        copy.wait()
    for at in range(topk):
        group = DECAY_RATE * rows[2 * at] + rows[2 * at + 1]
        one = jnp.sum(jnp.where(row_of == picks[at] % 8, group, 0.0), axis=0, keepdims=True)
        values = jnp.where(row_of == at, one, values)
        names = jnp.where(pick_row == at, picks[at].astype(jnp.float32), names)
    for replica in range(payload.shape[0]):
        payload[replica, :, :block] = values
        payload[replica, :, block:] = names
    for copy in staged:
        copy.wait()


def choose(picks, error, grad, momentum, params, replicas):
    blocks, block = params.shape
    topk = picks.shape[1]
    vmem = pl.BlockSpec(memory_space=pltpu.VMEM)
    hbm = pl.BlockSpec(memory_space=pltpu.HBM)
    picks, error, grad, momentum, params = (
        pltpu.with_memory_space_constraint(array, pltpu.HBM)
        for array in (picks, error, grad, momentum, params)
    )
    return pl.pallas_call(
        choose_kernel,
        out_shape=(
            jax.ShapeDtypeStruct((replicas, topk, block + LANES), jnp.float32),
            jax.ShapeDtypeStruct((blocks, block), jnp.float32),
            jax.ShapeDtypeStruct((blocks, block), jnp.float32),
        ),
        in_specs=[hbm] * 5,
        out_specs=(vmem,) * 3,
        scratch_shapes=[
            pltpu.SMEM((1, topk), jnp.int32),
            pltpu.VMEM((2 * topk, 8, block), jnp.float32),
            pltpu.SemaphoreType.DMA((2 * topk + 3,)),
        ],
        compiler_params=pltpu.CompilerParams(vmem_limit_bytes=VMEM_LIMIT),
        cost_estimate=pl.CostEstimate(flops=10**5, bytes_accessed=2 * 10**6, transcendentals=0),
    )(picks, error, grad, momentum, params)


def keep_kernel(picks_hbm, error_hbm, grad_hbm, new_error, picks_smem, error, grad, sems):
    copies = [
        pltpu.make_async_copy(picks_hbm, picks_smem, sems.at[0]),
        pltpu.make_async_copy(error_hbm, error, sems.at[1]),
        pltpu.make_async_copy(grad_hbm, grad, sems.at[2]),
    ]
    for copy in copies:
        copy.start()
    for copy in copies:
        copy.wait()
    row = lax.broadcasted_iota(jnp.int32, error.shape, 0)
    chosen = row == picks_smem[0, 0]
    for at in range(1, picks_smem.shape[1]):
        chosen = chosen | (row == picks_smem[0, at])
    new_error[...] = jnp.where(chosen, 0.0, DECAY_RATE * error[...] + grad[...])


def keep(picks, error, grad):
    hbm = pl.BlockSpec(memory_space=pltpu.HBM)
    picks, error, grad = (
        pltpu.with_memory_space_constraint(array, pltpu.HBM) for array in (picks, error, grad)
    )
    return pl.pallas_call(
        keep_kernel,
        out_shape=jax.ShapeDtypeStruct(error.shape, jnp.float32),
        in_specs=[hbm] * 3,
        out_specs=pl.BlockSpec(memory_space=pltpu.VMEM),
        scratch_shapes=[
            pltpu.SMEM(picks.shape, jnp.int32),
            pltpu.VMEM(error.shape, jnp.float32),
            pltpu.VMEM(error.shape, jnp.float32),
            pltpu.SemaphoreType.DMA((3,)),
        ],
        compiler_params=pltpu.CompilerParams(vmem_limit_bytes=VMEM_LIMIT),
        cost_estimate=pl.CostEstimate(flops=10**6, bytes_accessed=2 * 10**6, transcendentals=0),
    )(picks, error, grad)


def step(everyone, momentum, params):
    blocks, block = params.shape
    entries = everyone.shape[0]
    values = everyone[:, :block]
    picks = everyone[:, block:]
    lane = lax.broadcasted_iota(jnp.int32, (entries, LANES), 1).astype(jnp.float32)
    spread = jnp.concatenate(
        [(picks == lane + float(at)).astype(jnp.bfloat16) for at in range(0, blocks, LANES)], axis=1
    )
    delta = jnp.zeros((blocks, block), jnp.float32)
    rest = values
    for _ in range(3):
        part = rest.astype(jnp.bfloat16)
        rest = rest - part.astype(jnp.float32)
        delta += lax.dot_general(
            spread, part, (((0,), (0,)), ((), ())), preferred_element_type=jnp.float32
        )
    delta = delta / 16.0
    momentum_now = MOMENTUM_COEF * momentum[...] + delta
    return params[...] - STEP_SCALE * (delta + MOMENTUM_COEF * momentum_now), momentum_now


def shard_kernel(everyone, momentum, params, shard):
    shard[...] = step(everyone, momentum, params)[0].astype(jnp.bfloat16)


def state_kernel(everyone, momentum, params, new_params, new_momentum):
    new_params[...], new_momentum[...] = step(everyone, momentum, params)


def update(kernel, everyone, momentum, params, dtypes):
    vmem = pl.BlockSpec(memory_space=pltpu.VMEM)
    return pl.pallas_call(
        kernel,
        out_shape=[jax.ShapeDtypeStruct(params.shape, dtype) for dtype in dtypes],
        in_specs=[vmem] * 3,
        out_specs=[vmem] * len(dtypes),
        compiler_params=pltpu.CompilerParams(vmem_limit_bytes=VMEM_LIMIT),
        cost_estimate=pl.CostEstimate(flops=10**8, bytes_accessed=3 * 10**6, transcendentals=0),
    )(everyone, momentum, params)


def put(whole, pieces, shape, dtype):
    arrays = []
    for piece in pieces:
        if not any(piece[0] is a for a in arrays):
            arrays.append(piece[0])
    slots = [next(i for i, a in enumerate(arrays) if a is piece[0]) for piece in pieces]
    given = [] if whole is None else [whole]

    def kernel(*refs):
        sources = refs[len(given) : len(given) + len(arrays)]
        out, sems = refs[-2:]
        x, y, z, core = place_of_self()
        copies = []
        for (_, first, count, place, offsets, other), slot in zip(pieces, slots):
            by = 1 - core if other else core
            dx, dy, dz = (one + (two - one) * by for one, two in zip(*offsets))
            x_there = (x + dx + NX) % NX
            colour = colour_of(x_there, y + dy + NY, z + dz + NZ)
            own = x_there // 2
            for at in range(count):
                x_hi = 1 - own if (place + at) % 2 else own
                from_core = 1 - by if place + at >= 2 else by
                copies.append(
                    pltpu.make_async_copy(
                        sources[slot].at[first + at],
                        out.at[x_hi * NZ + z_of(colour, x_hi, from_core), from_core],
                        sems.at[len(copies)],
                    )
                )
        for copy in copies:
            copy.start()
        for copy in copies:
            copy.wait()

    total = sum(piece[2] for piece in pieces)
    return pl.pallas_call(
        kernel,
        out_shape=jax.ShapeDtypeStruct(shape, dtype),
        in_specs=[pl.BlockSpec(memory_space=pltpu.HBM)] * len(given)
        + [pl.BlockSpec(memory_space=pltpu.VMEM)] * len(arrays),
        out_specs=pl.BlockSpec(memory_space=pltpu.HBM),
        scratch_shapes=[pltpu.SemaphoreType.DMA((total,))],
        input_output_aliases={0: 0} if given else {},
        compiler_params=pltpu.CompilerParams(vmem_limit_bytes=VMEM_LIMIT),
        cost_estimate=pl.CostEstimate(
            flops=0, bytes_accessed=4 * total * shape[2] * shape[3], transcendentals=0
        ),
    )(*given, *arrays)


HERE = ((0, 0, 0), (0, 0, 0))
X = ((1, 0, 0), (-1, 0, 0))
XX = ((2, 0, 0), (-2, 0, 0))
Y = ((0, 1, 0), (0, -1, 0))
Z = ((0, 0, 1), (0, 0, -1))


def gather_slab(shard, aside):
    shape = (CLASSES, CORES, *shard.shape)
    own, partners = collect(shard, partner=False), collect(shard, partner=True)
    own, partners, aside = lax.optimization_barrier((own, partners, aside))
    half = jnp.stack([own, partners])
    near_x = fetch(half, X)
    portion = jnp.concatenate([half, swap(half)], axis=0)
    near_y, near_z = fetch(portion, Y), fetch(portion, Z)
    far_x = fetch(jnp.concatenate(lax.optimization_barrier((portion[2:], near_x)), axis=0), X)
    whole = put(None, [(portion, 0, 4, 0, HERE, False)], shape, shard.dtype)
    pieces = [(near_x, 0, 2, 0, X, False)]
    for array, offsets in ((near_y, Y), (near_z, Z)):
        pieces += [(array, 0, 4, 0, offsets, False), (swap(array[:2]), 0, 2, 0, offsets, True)]
    whole = put(whole, pieces, shape, shard.dtype)
    near_x, near_y, near_z, far_x, whole = lax.optimization_barrier(
        (near_x, near_y, near_z, far_x, whole)
    )
    rest = swap(jnp.concatenate([near_x, near_y[2:], near_z[2:]], axis=0))
    far_there = swap(far_x)
    for pieces in (
        [(far_x, 0, 2, 2, X, False), (far_x, 2, 2, 0, XX, False)],
        [(rest, 0, 2, 0, X, True), (rest, 2, 2, 2, Y, True), (rest, 4, 2, 2, Z, True)],
        [(far_there, 0, 2, 2, X, True), (far_there, 2, 2, 0, XX, True)],
    ):
        whole = put(whole, pieces, shape, shard.dtype)
    return whole, aside


def per_device(pseudo_grad, error_buf, momentum, params, picks):
    blocks, block = params.shape
    replicas = lax.axis_size("rep")
    payload, momentum_near, params_near = choose(
        picks, error_buf[0], pseudo_grad[0], momentum, params, replicas
    )
    everyone = lax.all_to_all(payload, "rep", 0, 0).reshape(-1, payload.shape[-1])
    (shard,) = update(shard_kernel, everyone, momentum_near, params_near, [jnp.bfloat16])
    error_buf, pseudo_grad, everyone, shard = lax.optimization_barrier(
        (error_buf, pseudo_grad, everyone, shard)
    )
    new_error = keep(picks, error_buf[0], pseudo_grad[0])[None]
    state = update(state_kernel, everyone, momentum_near, params_near, [jnp.float32] * 2)
    gathered, (new_error, new_params, new_momentum) = gather_slab(shard, (new_error, *state))
    return (new_params, new_momentum, new_error, gathered.reshape(-1, block))


def solution(mesh):
    in_specs = (
        P("rep", "fsdp", None),
        P("rep", "fsdp", None),
        P("fsdp", None),
        P("fsdp", None),
        P("rep", "fsdp"),
    )
    out_specs = (P("fsdp", None), P("fsdp", None), P("rep", "fsdp", None), P())
    return jax.shard_map(
        per_device, mesh=mesh, in_specs=in_specs, out_specs=out_specs, check_vma=False
    )
```

```python
import jax
import jax.numpy as jnp
from jax import lax
from jax.experimental import pallas as pl
from jax.experimental.pallas import tpu as pltpu
from jax.sharding import PartitionSpec as P

DECAY_RATE = 0.95
MOMENTUM_COEF = 0.9
STEP_SCALE = 0.7
LANES = 128
AXES = ("rep", "fsdp")
NX, NY, NZ, CORES = 4, 8, 8, 2
CLASSES = 2 * NZ
COLOURS = 8
VMEM_LIMIT = 40 * 1024 * 1024


def z_of(colour, x_hi, core):
    return (colour + 1 + 4 * core - x_hi + NZ) % NZ


def device_at(x, y, z, core):
    x, y, z, core = x % NX, y % NY, z % NZ, core % CORES
    return (y * 2 + x % 2) * (2 * NZ * CORES) + (x // 2) * (NZ * CORES) + z * CORES + core


PLACES = [
    (x, y, z, core) for x in range(NX) for y in range(NY) for z in range(NZ) for core in range(CORES)
]


def fetch(value, offsets):
    pairs = []
    for x, y, z, core in PLACES:
        dx, dy, dz = offsets[core]
        pairs.append((device_at(x + dx, y + dy, z + dz, core), device_at(x, y, z, core)))
    return lax.ppermute(value, AXES, pairs)


def swap(value):
    pairs = [(device_at(x, y, z, 1 - core), device_at(x, y, z, core)) for x, y, z, core in PLACES]
    return lax.ppermute(value, AXES, pairs)


def collect(shard, partner):
    pairs = []
    for x, y, z, core in PLACES:
        x_there = NX - 1 - x if partner else x
        z_there = z_of(colour_of(x, y, z), x_there // 2, core)
        pairs.append((device_at(x_there, y, z_there, core), device_at(x, y, z, core)))
    return lax.ppermute(shard, AXES, pairs)


def place_of_self():
    rep, shard = lax.axis_index("rep"), lax.axis_index("fsdp")
    x = (shard // (NZ * CORES)) * 2 + rep % 2
    return x, rep // 2, (shard // CORES) % NZ, shard % CORES


def colour_of(x, y, z):
    return (2 * x + y + 3 * z) % COLOURS


def choose_kernel(
    picks_hbm, error, grad, momentum, params, payload, momentum_near, params_near, picks_smem, rows, sems
):
    topk, block = payload.shape[1], error.shape[1]
    staged = [
        pltpu.make_async_copy(momentum, momentum_near, sems.at[2 * topk]),
        pltpu.make_async_copy(params, params_near, sems.at[2 * topk + 1]),
    ]
    names_load = pltpu.make_async_copy(picks_hbm, picks_smem, sems.at[2 * topk + 2])
    names_load.start()
    for copy in staged:
        copy.start()
    names_load.wait()
    picks = [picks_smem[0, at] for at in range(topk)]
    loads = []
    for at in range(topk):
        first = pl.multiple_of((picks[at] // 8) * 8, 8)
        for which, array in enumerate((error, grad)):
            slot = 2 * at + which
            loads.append(
                pltpu.make_async_copy(array.at[pl.ds(first, 8)], rows.at[slot], sems.at[slot])
            )
    for copy in loads:
        copy.start()
    row_of = lax.broadcasted_iota(jnp.int32, (8, block), 0)
    pick_row = lax.broadcasted_iota(jnp.int32, (topk, LANES), 0)
    values = jnp.zeros((topk, block), jnp.float32)
    names = jnp.zeros((topk, LANES), jnp.float32)
    for copy in loads:
        copy.wait()
    for at in range(topk):
        group = DECAY_RATE * rows[2 * at] + rows[2 * at + 1]
        one = jnp.sum(jnp.where(row_of == picks[at] % 8, group, 0.0), axis=0, keepdims=True)
        values = jnp.where(row_of == at, one, values)
        names = jnp.where(pick_row == at, picks[at].astype(jnp.float32), names)
    for replica in range(payload.shape[0]):
        payload[replica, :, :block] = values
        payload[replica, :, block:] = names
    for copy in staged:
        copy.wait()


def choose(picks, error, grad, momentum, params, replicas):
    blocks, block = params.shape
    topk = picks.shape[1]
    vmem = pl.BlockSpec(memory_space=pltpu.VMEM)
    hbm = pl.BlockSpec(memory_space=pltpu.HBM)
    picks, error, grad, momentum, params = (
        pltpu.with_memory_space_constraint(array, pltpu.HBM)
        for array in (picks, error, grad, momentum, params)
    )
    return pl.pallas_call(
        choose_kernel,
        out_shape=(
            jax.ShapeDtypeStruct((replicas, topk, block + LANES), jnp.float32),
            jax.ShapeDtypeStruct((blocks, block), jnp.float32),
            jax.ShapeDtypeStruct((blocks, block), jnp.float32),
        ),
        in_specs=[hbm] * 5,
        out_specs=(vmem,) * 3,
        scratch_shapes=[
            pltpu.SMEM((1, topk), jnp.int32),
            pltpu.VMEM((2 * topk, 8, block), jnp.float32),
            pltpu.SemaphoreType.DMA((2 * topk + 3,)),
        ],
        compiler_params=pltpu.CompilerParams(vmem_limit_bytes=VMEM_LIMIT),
        cost_estimate=pl.CostEstimate(flops=10**5, bytes_accessed=2 * 10**6, transcendentals=0),
    )(picks, error, grad, momentum, params)


def keep_kernel(picks_hbm, error_hbm, grad_hbm, new_error, picks_smem, error, grad, sems):
    copies = [
        pltpu.make_async_copy(picks_hbm, picks_smem, sems.at[0]),
        pltpu.make_async_copy(error_hbm, error, sems.at[1]),
        pltpu.make_async_copy(grad_hbm, grad, sems.at[2]),
    ]
    for copy in copies:
        copy.start()
    for copy in copies:
        copy.wait()
    row = lax.broadcasted_iota(jnp.int32, error.shape, 0)
    chosen = row == picks_smem[0, 0]
    for at in range(1, picks_smem.shape[1]):
        chosen = chosen | (row == picks_smem[0, at])
    new_error[...] = jnp.where(chosen, 0.0, DECAY_RATE * error[...] + grad[...])


def keep(picks, error, grad):
    hbm = pl.BlockSpec(memory_space=pltpu.HBM)
    picks, error, grad = (
        pltpu.with_memory_space_constraint(array, pltpu.HBM) for array in (picks, error, grad)
    )
    return pl.pallas_call(
        keep_kernel,
        out_shape=jax.ShapeDtypeStruct(error.shape, jnp.float32),
        in_specs=[hbm] * 3,
        out_specs=pl.BlockSpec(memory_space=pltpu.VMEM),
        scratch_shapes=[
            pltpu.SMEM(picks.shape, jnp.int32),
            pltpu.VMEM(error.shape, jnp.float32),
            pltpu.VMEM(error.shape, jnp.float32),
            pltpu.SemaphoreType.DMA((3,)),
        ],
        compiler_params=pltpu.CompilerParams(vmem_limit_bytes=VMEM_LIMIT),
        cost_estimate=pl.CostEstimate(flops=10**6, bytes_accessed=2 * 10**6, transcendentals=0),
    )(picks, error, grad)


def step(everyone, momentum, params):
    blocks, block = params.shape
    entries = everyone.shape[0]
    values = everyone[:, :block]
    picks = everyone[:, block:]
    lane = lax.broadcasted_iota(jnp.int32, (entries, LANES), 1).astype(jnp.float32)
    spread = jnp.concatenate(
        [(picks == lane + float(at)).astype(jnp.bfloat16) for at in range(0, blocks, LANES)], axis=1
    )
    delta = jnp.zeros((blocks, block), jnp.float32)
    rest = values
    for _ in range(3):
        part = rest.astype(jnp.bfloat16)
        rest = rest - part.astype(jnp.float32)
        delta += lax.dot_general(
            spread, part, (((0,), (0,)), ((), ())), preferred_element_type=jnp.float32
        )
    delta = delta / 16.0
    momentum_now = MOMENTUM_COEF * momentum[...] + delta
    return params[...] - STEP_SCALE * (delta + MOMENTUM_COEF * momentum_now), momentum_now


def shard_kernel(everyone, momentum, params, shard):
    shard[...] = step(everyone, momentum, params)[0].astype(jnp.bfloat16)


def state_kernel(everyone, momentum, params, new_params, new_momentum):
    new_params[...], new_momentum[...] = step(everyone, momentum, params)


def update(kernel, everyone, momentum, params, dtypes):
    vmem = pl.BlockSpec(memory_space=pltpu.VMEM)
    return pl.pallas_call(
        kernel,
        out_shape=[jax.ShapeDtypeStruct(params.shape, dtype) for dtype in dtypes],
        in_specs=[vmem] * 3,
        out_specs=[vmem] * len(dtypes),
        compiler_params=pltpu.CompilerParams(vmem_limit_bytes=VMEM_LIMIT),
        cost_estimate=pl.CostEstimate(flops=10**8, bytes_accessed=3 * 10**6, transcendentals=0),
    )(everyone, momentum, params)


def put(whole, pieces, shape, dtype):
    arrays = []
    for piece in pieces:
        if not any(piece[0] is a for a in arrays):
            arrays.append(piece[0])
    slots = [next(i for i, a in enumerate(arrays) if a is piece[0]) for piece in pieces]
    given = [] if whole is None else [whole]

    def kernel(*refs):
        sources = refs[len(given) : len(given) + len(arrays)]
        out, sems = refs[-2:]
        x, y, z, core = place_of_self()
        copies = []
        for (_, first, count, place, offsets, other), slot in zip(pieces, slots):
            by = 1 - core if other else core
            dx, dy, dz = (one + (two - one) * by for one, two in zip(*offsets))
            x_there = (x + dx + NX) % NX
            colour = colour_of(x_there, y + dy + NY, z + dz + NZ)
            own = x_there // 2
            for at in range(count):
                x_hi = 1 - own if (place + at) % 2 else own
                from_core = 1 - by if place + at >= 2 else by
                copies.append(
                    pltpu.make_async_copy(
                        sources[slot].at[first + at],
                        out.at[x_hi * NZ + z_of(colour, x_hi, from_core), from_core],
                        sems.at[len(copies)],
                    )
                )
        for copy in copies:
            copy.start()
        for copy in copies:
            copy.wait()

    total = sum(piece[2] for piece in pieces)
    return pl.pallas_call(
        kernel,
        out_shape=jax.ShapeDtypeStruct(shape, dtype),
        in_specs=[pl.BlockSpec(memory_space=pltpu.HBM)] * len(given)
        + [pl.BlockSpec(memory_space=pltpu.VMEM)] * len(arrays),
        out_specs=pl.BlockSpec(memory_space=pltpu.HBM),
        scratch_shapes=[pltpu.SemaphoreType.DMA((total,))],
        input_output_aliases={0: 0} if given else {},
        compiler_params=pltpu.CompilerParams(vmem_limit_bytes=VMEM_LIMIT),
        cost_estimate=pl.CostEstimate(
            flops=0, bytes_accessed=4 * total * shape[2] * shape[3], transcendentals=0
        ),
    )(*given, *arrays)


HERE = ((0, 0, 0), (0, 0, 0))
X = ((1, 0, 0), (-1, 0, 0))
XX = ((2, 0, 0), (-2, 0, 0))
Y = ((0, 1, 0), (0, -1, 0))
Z = ((0, 0, 1), (0, 0, -1))


def gather_slab(shard, aside):
    shape = (CLASSES, CORES, *shard.shape)
    own, partners = collect(shard, partner=False), collect(shard, partner=True)
    own, partners, aside = lax.optimization_barrier((own, partners, aside))
    half = jnp.stack([own, partners])
    near_x = fetch(half, X)
    portion = jnp.concatenate([half, swap(half)], axis=0)
    near_y, near_z = fetch(portion, Y), fetch(portion, Z)
    far_x = fetch(jnp.concatenate(lax.optimization_barrier((portion[2:], near_x)), axis=0), X)
    pieces = [(portion, 0, 4, 0, HERE, False), (near_x, 0, 2, 0, X, False)]
    whole = put(None, pieces, shape, shard.dtype)
    near_y, whole = lax.optimization_barrier((near_y, whole))
    pieces = []
    for array, offsets in ((near_y, Y), (near_z, Z)):
        pieces += [(array, 0, 4, 0, offsets, False), (swap(array[:2]), 0, 2, 0, offsets, True)]
    whole = put(whole, pieces, shape, shard.dtype)
    near_x, near_y, near_z, far_x, whole = lax.optimization_barrier(
        (near_x, near_y, near_z, far_x, whole)
    )
    rest = swap(jnp.concatenate([near_x, near_y[2:], near_z[2:]], axis=0))
    far_there = swap(far_x)
    for pieces in (
        [(far_x, 0, 2, 2, X, False), (far_x, 2, 2, 0, XX, False)],
        [(rest, 0, 2, 0, X, True), (rest, 2, 2, 2, Y, True), (rest, 4, 2, 2, Z, True)],
        [(far_there, 0, 2, 2, X, True), (far_there, 2, 2, 0, XX, True)],
    ):
        whole = put(whole, pieces, shape, shard.dtype)
    return whole, aside


def per_device(pseudo_grad, error_buf, momentum, params, picks):
    blocks, block = params.shape
    replicas = lax.axis_size("rep")
    payload, momentum_near, params_near = choose(
        picks, error_buf[0], pseudo_grad[0], momentum, params, replicas
    )
    everyone = lax.all_to_all(payload, "rep", 0, 0).reshape(-1, payload.shape[-1])
    (shard,) = update(shard_kernel, everyone, momentum_near, params_near, [jnp.bfloat16])
    error_buf, pseudo_grad, everyone, shard = lax.optimization_barrier(
        (error_buf, pseudo_grad, everyone, shard)
    )
    new_error = keep(picks, error_buf[0], pseudo_grad[0])[None]
    state = update(state_kernel, everyone, momentum_near, params_near, [jnp.float32] * 2)
    gathered, (new_error, new_params, new_momentum) = gather_slab(shard, (new_error, *state))
    return (new_params, new_momentum, new_error, gathered.reshape(-1, block))


def solution(mesh):
    in_specs = (
        P("rep", "fsdp", None),
        P("rep", "fsdp", None),
        P("fsdp", None),
        P("fsdp", None),
        P("rep", "fsdp"),
    )
    out_specs = (P("fsdp", None), P("fsdp", None), P("rep", "fsdp", None), P())
    return jax.shard_map(
        per_device, mesh=mesh, in_specs=in_specs, out_specs=out_specs, check_vma=False
    )
```

```python
import jax
import jax.numpy as jnp
from jax import lax
from jax.experimental import pallas as pl
from jax.experimental.pallas import tpu as pltpu
from jax.sharding import PartitionSpec as P

DECAY_RATE = 0.95
MOMENTUM_COEF = 0.9
STEP_SCALE = 0.7
LANES = 128
AXES = ("rep", "fsdp")
NX, NY, NZ, CORES = 4, 8, 8, 2
CLASSES = 2 * NZ
COLOURS = 8
VMEM_LIMIT = 40 * 1024 * 1024


def z_of(colour, x_hi, core):
    return (colour + 1 + 4 * core - x_hi + NZ) % NZ


def device_at(x, y, z, core):
    x, y, z, core = x % NX, y % NY, z % NZ, core % CORES
    return (y * 2 + x % 2) * (2 * NZ * CORES) + (x // 2) * (NZ * CORES) + z * CORES + core


PLACES = [
    (x, y, z, core) for x in range(NX) for y in range(NY) for z in range(NZ) for core in range(CORES)
]


def fetch(value, offsets):
    pairs = []
    for x, y, z, core in PLACES:
        dx, dy, dz = offsets[core]
        pairs.append((device_at(x + dx, y + dy, z + dz, core), device_at(x, y, z, core)))
    return lax.ppermute(value, AXES, pairs)


def swap(value):
    pairs = [(device_at(x, y, z, 1 - core), device_at(x, y, z, core)) for x, y, z, core in PLACES]
    return lax.ppermute(value, AXES, pairs)


def collect(shard, partner):
    pairs = []
    for x, y, z, core in PLACES:
        x_there = NX - 1 - x if partner else x
        z_there = z_of(colour_of(x, y, z), x_there // 2, core)
        pairs.append((device_at(x_there, y, z_there, core), device_at(x, y, z, core)))
    return lax.ppermute(shard, AXES, pairs)


def place_of_self():
    rep, shard = lax.axis_index("rep"), lax.axis_index("fsdp")
    x = (shard // (NZ * CORES)) * 2 + rep % 2
    return x, rep // 2, (shard // CORES) % NZ, shard % CORES


def colour_of(x, y, z):
    return (2 * x + y + 3 * z) % COLOURS


def choose_kernel(
    picks_hbm, error, grad, momentum, params, payload, momentum_near, params_near, picks_smem, rows, sems
):
    topk, block = payload.shape[1], error.shape[1]
    staged = [
        pltpu.make_async_copy(momentum, momentum_near, sems.at[2 * topk]),
        pltpu.make_async_copy(params, params_near, sems.at[2 * topk + 1]),
    ]
    names_load = pltpu.make_async_copy(picks_hbm, picks_smem, sems.at[2 * topk + 2])
    names_load.start()
    for copy in staged:
        copy.start()
    names_load.wait()
    picks = [picks_smem[0, at] for at in range(topk)]
    loads = []
    for at in range(topk):
        first = pl.multiple_of((picks[at] // 8) * 8, 8)
        for which, array in enumerate((error, grad)):
            slot = 2 * at + which
            loads.append(
                pltpu.make_async_copy(array.at[pl.ds(first, 8)], rows.at[slot], sems.at[slot])
            )
    for copy in loads:
        copy.start()
    row_of = lax.broadcasted_iota(jnp.int32, (8, block), 0)
    pick_row = lax.broadcasted_iota(jnp.int32, (topk, LANES), 0)
    values = jnp.zeros((topk, block), jnp.float32)
    names = jnp.zeros((topk, LANES), jnp.float32)
    for copy in loads:
        copy.wait()
    for at in range(topk):
        group = DECAY_RATE * rows[2 * at] + rows[2 * at + 1]
        one = jnp.sum(jnp.where(row_of == picks[at] % 8, group, 0.0), axis=0, keepdims=True)
        values = jnp.where(row_of == at, one, values)
        names = jnp.where(pick_row == at, picks[at].astype(jnp.float32), names)
    for replica in range(payload.shape[0]):
        payload[replica, :, :block] = values
        payload[replica, :, block:] = names
    for copy in staged:
        copy.wait()


def choose(picks, error, grad, momentum, params, replicas):
    blocks, block = params.shape
    topk = picks.shape[1]
    vmem = pl.BlockSpec(memory_space=pltpu.VMEM)
    hbm = pl.BlockSpec(memory_space=pltpu.HBM)
    picks, error, grad, momentum, params = (
        pltpu.with_memory_space_constraint(array, pltpu.HBM)
        for array in (picks, error, grad, momentum, params)
    )
    return pl.pallas_call(
        choose_kernel,
        out_shape=(
            jax.ShapeDtypeStruct((replicas, topk, block + LANES), jnp.float32),
            jax.ShapeDtypeStruct((blocks, block), jnp.float32),
            jax.ShapeDtypeStruct((blocks, block), jnp.float32),
        ),
        in_specs=[hbm] * 5,
        out_specs=(vmem,) * 3,
        scratch_shapes=[
            pltpu.SMEM((1, topk), jnp.int32),
            pltpu.VMEM((2 * topk, 8, block), jnp.float32),
            pltpu.SemaphoreType.DMA((2 * topk + 3,)),
        ],
        compiler_params=pltpu.CompilerParams(vmem_limit_bytes=VMEM_LIMIT),
        cost_estimate=pl.CostEstimate(flops=10**5, bytes_accessed=2 * 10**6, transcendentals=0),
    )(picks, error, grad, momentum, params)


def keep_kernel(picks_hbm, error_hbm, grad_hbm, new_error, picks_smem, error, grad, sems):
    copies = [
        pltpu.make_async_copy(picks_hbm, picks_smem, sems.at[0]),
        pltpu.make_async_copy(error_hbm, error, sems.at[1]),
        pltpu.make_async_copy(grad_hbm, grad, sems.at[2]),
    ]
    for copy in copies:
        copy.start()
    for copy in copies:
        copy.wait()
    row = lax.broadcasted_iota(jnp.int32, error.shape, 0)
    chosen = row == picks_smem[0, 0]
    for at in range(1, picks_smem.shape[1]):
        chosen = chosen | (row == picks_smem[0, at])
    new_error[...] = jnp.where(chosen, 0.0, DECAY_RATE * error[...] + grad[...])


def keep(picks, error, grad):
    hbm = pl.BlockSpec(memory_space=pltpu.HBM)
    picks, error, grad = (
        pltpu.with_memory_space_constraint(array, pltpu.HBM) for array in (picks, error, grad)
    )
    return pl.pallas_call(
        keep_kernel,
        out_shape=jax.ShapeDtypeStruct(error.shape, jnp.float32),
        in_specs=[hbm] * 3,
        out_specs=pl.BlockSpec(memory_space=pltpu.VMEM),
        scratch_shapes=[
            pltpu.SMEM(picks.shape, jnp.int32),
            pltpu.VMEM(error.shape, jnp.float32),
            pltpu.VMEM(error.shape, jnp.float32),
            pltpu.SemaphoreType.DMA((3,)),
        ],
        compiler_params=pltpu.CompilerParams(vmem_limit_bytes=VMEM_LIMIT),
        cost_estimate=pl.CostEstimate(flops=10**6, bytes_accessed=2 * 10**6, transcendentals=0),
    )(picks, error, grad)


def step(everyone, momentum, params):
    blocks, block = params.shape
    entries = everyone.shape[0]
    values = everyone[:, :block]
    picks = everyone[:, block:]
    lane = lax.broadcasted_iota(jnp.int32, (entries, LANES), 1).astype(jnp.float32)
    spread = jnp.concatenate(
        [(picks == lane + float(at)).astype(jnp.bfloat16) for at in range(0, blocks, LANES)], axis=1
    )
    delta = jnp.zeros((blocks, block), jnp.float32)
    rest = values
    for _ in range(3):
        part = rest.astype(jnp.bfloat16)
        rest = rest - part.astype(jnp.float32)
        delta += lax.dot_general(
            spread, part, (((0,), (0,)), ((), ())), preferred_element_type=jnp.float32
        )
    delta = delta / 16.0
    momentum_now = MOMENTUM_COEF * momentum[...] + delta
    return params[...] - STEP_SCALE * (delta + MOMENTUM_COEF * momentum_now), momentum_now


def shard_kernel(everyone, momentum, params, shard):
    shard[...] = step(everyone, momentum, params)[0].astype(jnp.bfloat16)


def state_kernel(everyone, momentum, params, new_params, new_momentum):
    new_params[...], new_momentum[...] = step(everyone, momentum, params)


def update(kernel, everyone, momentum, params, dtypes):
    vmem = pl.BlockSpec(memory_space=pltpu.VMEM)
    return pl.pallas_call(
        kernel,
        out_shape=[jax.ShapeDtypeStruct(params.shape, dtype) for dtype in dtypes],
        in_specs=[vmem] * 3,
        out_specs=[vmem] * len(dtypes),
        compiler_params=pltpu.CompilerParams(vmem_limit_bytes=VMEM_LIMIT),
        cost_estimate=pl.CostEstimate(flops=10**8, bytes_accessed=3 * 10**6, transcendentals=0),
    )(everyone, momentum, params)


def put(whole, pieces, shape, dtype):
    arrays = []
    for piece in pieces:
        if not any(piece[0] is a for a in arrays):
            arrays.append(piece[0])
    slots = [next(i for i, a in enumerate(arrays) if a is piece[0]) for piece in pieces]
    given = [] if whole is None else [whole]

    def kernel(*refs):
        sources = refs[len(given) : len(given) + len(arrays)]
        out, sems = refs[-2:]
        x, y, z, core = place_of_self()
        copies = []
        for (_, first, count, place, offsets, other), slot in zip(pieces, slots):
            by = 1 - core if other else core
            dx, dy, dz = (one + (two - one) * by for one, two in zip(*offsets))
            x_there = (x + dx + NX) % NX
            colour = colour_of(x_there, y + dy + NY, z + dz + NZ)
            own = x_there // 2
            for at in range(count):
                x_hi = 1 - own if (place + at) % 2 else own
                from_core = 1 - by if place + at >= 2 else by
                copies.append(
                    pltpu.make_async_copy(
                        sources[slot].at[first + at],
                        out.at[x_hi * NZ + z_of(colour, x_hi, from_core), from_core],
                        sems.at[len(copies)],
                    )
                )
        for copy in copies:
            copy.start()
        for copy in copies:
            copy.wait()

    total = sum(piece[2] for piece in pieces)
    return pl.pallas_call(
        kernel,
        out_shape=jax.ShapeDtypeStruct(shape, dtype),
        in_specs=[pl.BlockSpec(memory_space=pltpu.HBM)] * len(given)
        + [pl.BlockSpec(memory_space=pltpu.VMEM)] * len(arrays),
        out_specs=pl.BlockSpec(memory_space=pltpu.HBM),
        scratch_shapes=[pltpu.SemaphoreType.DMA((total,))],
        input_output_aliases={0: 0} if given else {},
        compiler_params=pltpu.CompilerParams(vmem_limit_bytes=VMEM_LIMIT),
        cost_estimate=pl.CostEstimate(
            flops=0, bytes_accessed=4 * total * shape[2] * shape[3], transcendentals=0
        ),
    )(*given, *arrays)


HERE = ((0, 0, 0), (0, 0, 0))
X = ((1, 0, 0), (-1, 0, 0))
XX = ((2, 0, 0), (-2, 0, 0))
Y = ((0, 1, 0), (0, -1, 0))
Z = ((0, 0, 1), (0, 0, -1))


def gather_slab(shard, aside):
    shape = (CLASSES, CORES, *shard.shape)
    own, partners = collect(shard, partner=False), collect(shard, partner=True)
    own, partners, aside = lax.optimization_barrier((own, partners, aside))
    half = jnp.stack([own, partners])
    near_x = fetch(half, X)
    portion = jnp.concatenate([half, swap(half)], axis=0)
    near_y, near_z = fetch(portion, Y), fetch(portion, Z)
    far_x = fetch(jnp.concatenate(lax.optimization_barrier((portion[2:], near_x)), axis=0), X)
    pieces = [(portion, 0, 4, 0, HERE, False), (near_x, 0, 2, 0, X, False)]
    whole = put(None, pieces, shape, shard.dtype)
    near_y, whole = lax.optimization_barrier((near_y, whole))
    pieces = [(near_y, 0, 4, 0, Y, False), (swap(near_y[:2]), 0, 2, 0, Y, True)]
    whole = put(whole, [*pieces, (near_z, 0, 4, 0, Z, False)], shape, shard.dtype)
    near_z_there = swap(near_z[:2])
    near_x, near_y, near_z, near_z_there, far_x, whole = lax.optimization_barrier(
        (near_x, near_y, near_z, near_z_there, far_x, whole)
    )
    rest = swap(jnp.concatenate([near_x, near_y[2:], near_z[2:]], axis=0))
    far_there = swap(far_x)
    for pieces in (
        [(far_x, 0, 2, 2, X, False), (far_x, 2, 2, 0, XX, False), (near_z_there, 0, 2, 0, Z, True)],
        [(rest, 0, 2, 0, X, True), (rest, 2, 2, 2, Y, True), (rest, 4, 2, 2, Z, True)],
        [(far_there, 0, 2, 2, X, True), (far_there, 2, 2, 0, XX, True)],
    ):
        whole = put(whole, pieces, shape, shard.dtype)
    return whole, aside


def per_device(pseudo_grad, error_buf, momentum, params, picks):
    blocks, block = params.shape
    replicas = lax.axis_size("rep")
    payload, momentum_near, params_near = choose(
        picks, error_buf[0], pseudo_grad[0], momentum, params, replicas
    )
    everyone = lax.all_to_all(payload, "rep", 0, 0).reshape(-1, payload.shape[-1])
    (shard,) = update(shard_kernel, everyone, momentum_near, params_near, [jnp.bfloat16])
    error_buf, pseudo_grad, everyone, shard = lax.optimization_barrier(
        (error_buf, pseudo_grad, everyone, shard)
    )
    new_error = keep(picks, error_buf[0], pseudo_grad[0])[None]
    state = update(state_kernel, everyone, momentum_near, params_near, [jnp.float32] * 2)
    gathered, (new_error, new_params, new_momentum) = gather_slab(shard, (new_error, *state))
    return (new_params, new_momentum, new_error, gathered.reshape(-1, block))


def solution(mesh):
    in_specs = (
        P("rep", "fsdp", None),
        P("rep", "fsdp", None),
        P("fsdp", None),
        P("fsdp", None),
        P("rep", "fsdp"),
    )
    out_specs = (P("fsdp", None), P("fsdp", None), P("rep", "fsdp", None), P())
    return jax.shard_map(
        per_device, mesh=mesh, in_specs=in_specs, out_specs=out_specs, check_vma=False
    )
```
